256 devices in a mesh: grp: 8 (over y, core), tp: 16 (over z, x_hi), sec: 2 (over x_lo).
Axes of the slice: x: 4 (x_hi: 2, x_lo: 2; x = x_hi * 2 + x_lo), y: 4, z: 8, core: 2. Of those that a mesh axis runs over, the one named last changes fastest.
Arguments:
- layer_in: bfloat16 [2, 512, 4, 8192], P('sec', 'grp', None, 'tp'), may hold values from -6 to 6
- q_weight: bfloat16 [2, 8192, 8192], P('sec', 'grp', 'tp'), may hold values from -0.0625 to 0.0625
- kv_weight: bfloat16 [2, 8192, 2048], P('sec', 'grp', 'tp'), may hold values from -0.0625 to 0.0625
- o_weight: bfloat16 [2, 8192, 8192], P('sec', 'tp', 'grp'), may hold values from -0.5 to 0.5
- kv_cache: bfloat16 [2, 512, 4096, 256], P('sec', 'grp', 'tp'), may hold values from -600 to 600
- cache_lengths: int32 [512], P('grp'), may hold values from 1 to 512, as said below
- value_head: float32 [8192], P('tp'), may hold values from -0.0625 to 0.0625
Outputs:
- hidden_out: bfloat16 [2, 512, 4, 8192], P('sec', 'grp', None, 'tp')
- token_gap: float32 [512, 4], P('grp', 'sec')
The draws below stay inside these ranges and needn't reach their ends.
Inputs may be any that keep to these rules, and one draw needn't show every extreme that they name: `cache_lengths`: every rollout has at least one cached position; some rollout fills the whole cache and some holds a single position. Positions at or after a rollout's length hold arbitrary values.
All inputs are finite; a program needn't handle non-finite values.
Results may differ from the reference program's by a relative error of at most 0.018.
Values may be sent and summed in bfloat16 or wider, within the bound.
A program may use at most 128 MiB of HBM per device.

```python
import jax
import jax.numpy as jnp
from jax import lax

D = 8192
H = 64
KVH = 8
HD = 128
R_DEV = 64
CACHE = 512
NSTEP = 4
R = 512
N_GRP = 8


def draw_cache_lengths(key, part):
    first_key, second_key, third_key = jax.random.split(jax.random.fold_in(key, 11), 3)
    factor_a = jax.random.randint(first_key, (R,), 1, 17)
    factor_b = jax.random.randint(second_key, (R,), 1, 17)
    lengths = 1 + factor_a * factor_b * (CACHE - 1) // 256
    chosen = jax.random.randint(third_key, (), 0, R)
    index = jnp.arange(R)
    lengths = jnp.where(index == chosen, CACHE, lengths)
    lengths = jnp.where(index == (chosen + 1) % R, 1, lengths)
    return lengths.astype(jnp.int32)


def draw_kv_cache(key, part):
    base_key = jax.random.fold_in(jax.random.fold_in(key, 23), 0)
    shape = (2, R, KVH, CACHE, 2, HD)
    values = jnp.clip(jax.random.normal(base_key, shape, jnp.float32), -4.0, 4.0)
    return values.reshape(2, R, KVH * CACHE, 2 * HD).astype(jnp.bfloat16)


def levels(key, shape, cuts, smallest, top_value):
    loudness = 1.0
    for dim, shards_of in cuts:
        heights = jax.random.uniform(jax.random.fold_in(jax.random.fold_in(key, 6), dim), (shards_of,), jnp.float32, smallest / len(cuts), top_value / len(cuts))
        loudness = loudness * jnp.repeat(jnp.exp(heights), shape[dim] // shards_of).reshape((-1,) + (1,) * (len(shape) - 1 - dim))
    return loudness


def noise(rng, dims, width, limit, cuts=(), held_as=jnp.bfloat16):
    drawn = width * jax.random.normal(rng, dims, jnp.float32)
    if cuts:
        drawn = drawn * levels(rng, dims, cuts, -0.22, 0.18)
    return jnp.clip(drawn, -limit, limit).astype(held_as)


def setup_inputs(seed: int = 0) -> dict:
    key_list = jax.random.split(jax.random.key(seed), 8)
    layer_in = noise(key_list[0], (2, R, NSTEP, D), 1.0, 6.0, ((0, 2), (1, 8), (3, 16)))
    q_weight = noise(key_list[1], (2, D, H * HD), D ** -0.5, 0.0625, ((0, 2), (1, 8), (2, 16)))
    kv_weight = noise(key_list[2], (2, D, 2 * KVH * HD), D ** -0.5, 0.0625, ((0, 2), (1, 8), (2, 16)))
    o_weight = noise(key_list[3], (2, H * HD, D), (H * HD // 64) ** -0.5, 0.5, ((0, 2), (1, 16), (2, 8)))
    kv_cache = draw_kv_cache(jax.random.fold_in(key_list[7], 71), 0)
    cache_lengths = draw_cache_lengths(jax.random.fold_in(key_list[7], 71), 0)
    value_head = noise(key_list[6], (D,), D ** -0.5, 0.0625, ((0, 16),), jnp.float32)
    return {"layer_in": layer_in, "q_weight": q_weight, "kv_weight": kv_weight, "o_weight": o_weight, "kv_cache": kv_cache, "cache_lengths": cache_lengths, "value_head": value_head}


def rounded(values):
    return lax.optimization_barrier(values.astype(jnp.bfloat16)).astype(jnp.float32)


def attend(block):
    query, new_key, new_value, cache, lengths = block
    rows = query.shape[0]
    cache_f = cache.astype(jnp.float32).reshape(rows, KVH, CACHE, 2, HD)
    cache_keys = cache_f[:, :, :, 0, :]
    cache_vals = cache_f[:, :, :, 1, :]
    score_scale = HD ** -0.5
    cache_scores = jnp.einsum('rskgd,rkpd->rskgp', query, cache_keys) * score_scale
    new_scores = jnp.einsum('rskgd,rtkd->rskgt', query, new_key) * score_scale
    visible = (jnp.arange(CACHE)[None, :] < lengths[:, None])[:, None, None, None, :]
    causal = (jnp.arange(NSTEP)[None, :] <= jnp.arange(NSTEP)[:, None])[None, :, None, None, :]
    row_peak = jnp.maximum(jnp.max(jnp.where(visible, cache_scores, -1e30), axis=-1),
                           jnp.max(jnp.where(causal, new_scores, -1e30), axis=-1))
    cache_w = jnp.where(visible, jnp.exp(cache_scores - row_peak[..., None]), 0.0)
    new_w = jnp.where(causal, jnp.exp(new_scores - row_peak[..., None]), 0.0)
    row_total = jnp.sum(cache_w, axis=-1) + jnp.sum(new_w, axis=-1)
    weighted = jnp.einsum('rskgp,rkpd->rskgd', rounded(cache_w), cache_vals)
    weighted = weighted + jnp.einsum('rskgt,rtkd->rskgd', rounded(new_w), new_value)
    return (weighted / row_total[..., None]).astype(jnp.bfloat16)


def section(layer_x, wq, wkv, wo, cache, lengths):
    flat = layer_x.reshape(R * NSTEP, D)
    query = rounded(jnp.dot(flat, wq, preferred_element_type=jnp.float32))
    query = query.reshape(N_GRP, R_DEV, NSTEP, KVH, H // KVH, HD)
    new_kv = rounded(jnp.dot(flat, wkv, preferred_element_type=jnp.float32))
    new_kv = new_kv.reshape(N_GRP, R_DEV, NSTEP, KVH, 2, HD)
    blocks = (query, new_kv[:, :, :, :, 0, :], new_kv[:, :, :, :, 1, :],
              cache.reshape(N_GRP, R_DEV, KVH * CACHE, 2 * HD), lengths.reshape(N_GRP, R_DEV))
    context = lax.map(attend, blocks).reshape(R * NSTEP, H * HD)
    result = jnp.dot(context, wo, preferred_element_type=jnp.float32).astype(jnp.bfloat16)
    return result.reshape(R, NSTEP, D)


def reference(layer_in, q_weight, kv_weight, o_weight, kv_cache, cache_lengths, value_head):
    policy = section(layer_in[0], q_weight[0], kv_weight[0], o_weight[0], kv_cache[0], cache_lengths)
    refer = section(layer_in[1], q_weight[1], kv_weight[1], o_weight[1], kv_cache[1], cache_lengths)
    hidden_out = jnp.stack([policy, refer])
    diff = policy.astype(jnp.float32) - refer.astype(jnp.float32)
    token_gap = jnp.sum(diff * value_head, axis=-1)
    return hidden_out, token_gap
```

```python
import functools

import jax
import jax.numpy as jnp
from jax import lax
from jax.experimental import pallas as pl
from jax.experimental.pallas import tpu as pltpu
from jax.sharding import PartitionSpec as P

HD = 128
CACHE = 512
MESH = pl.DeviceIdType.MESH
BF = jnp.bfloat16
F32 = jnp.float32
MIB = 1024 * 1024


def dot(a, b):
    return jnp.dot(a, b, preferred_element_type=F32)


def dot_nt(a, b):
    return lax.dot_general(a, b, (((1,), (1,)), ((), ())), preferred_element_type=F32)


def remote(src, dst, send, recv, **where):
    return pltpu.make_async_remote_copy(
        src_ref=src, dst_ref=dst, send_sem=send, recv_sem=recv, device_id=where, device_id_type=MESH
    )


def places():
    grp, tp = lax.axis_index("grp"), lax.axis_index("tp")
    return grp, tp, grp // 2, grp % 2, tp // 2, tp % 2


class OutputWeights:
    def __init__(self, src, full, y_send, y_recv, c_send, c_recv, own_sem):
        grp, tp, y, c, z, xh = places()
        self.grp, self.c, self.y = grp, c, y
        self.right, self.left = 2 * ((y + 1) % 4) + c, 2 * ((y + 3) % 4) + c
        self.src, self.full = src, full
        self.y_send, self.y_recv, self.c_send, self.c_recv, self.own_sem = y_send, y_recv, c_send, c_recv, own_sem

    def to_core(self, slot, src, place):
        return remote(src, self.full.at[place], self.c_send.at[slot], self.c_recv.at[slot], grp=self.grp ^ 1)

    def from_core(self, slot, place):
        return remote(
            self.full.at[place], self.full.at[place ^ 1], self.c_send.at[slot], self.c_recv.at[slot], grp=self.grp ^ 1
        )

    def one(self, which, place, src=None):
        to = self.right if which == 0 else self.left
        return remote(
            self.full.at[place] if src is None else src, self.full.at[place],
            self.y_send.at[which], self.y_recv.at[which], grp=to,
        )

    def half(self, which, place):
        to = self.right if which == 0 else self.left
        rows = pl.ds(256 * which, 256)
        return remote(
            self.full.at[place, rows], self.full.at[place, rows],
            self.y_send.at[2 + which], self.y_recv.at[2 + which], grp=to,
        )

    def start(self):
        self.own = pltpu.make_async_copy(self.src, self.full.at[self.grp], self.own_sem)
        self.own.start()
        self.sent = [self.one(0, self.grp, self.src), self.one(1, self.grp, self.src), self.to_core(0, self.src, self.grp)]
        for copy in self.sent:
            copy.start()

    def middle(self):
        for which, place in ((0, self.left), (1, self.right)):
            self.one(which, place).wait_recv()
            ahead = self.half(which, place)
            ahead.start()
            over = self.to_core(1 + which, self.full.at[place], place)
            over.start()
            self.sent += [ahead, over]

    def last(self):
        far = 2 * ((self.y + 2) % 4) + self.c
        for which in (0, 1):
            self.half(which, far).wait_recv()
        over = self.to_core(3, self.full.at[far], far)
        over.start()
        self.sent.append(over)

    def finish(self):
        self.own.wait()
        for copy in self.sent:
            copy.wait_send()
        for slot in range(4):
            self.from_core(slot, self.grp).wait_recv()


def project_kernel(
    x_hbm, wq_hbm, wkv_hbm, wo_hbm, qkv_out, wo_own, wo_far,
    xs, ws, mine, keep, to_core, from_core, to_y, from_y, final,
    perm_send, perm_recv, r_send, r_recv, l_send, l_recv, w_local, w_send, w_recv,
    c_send, c_recv, y_send, y_recv, a_send, a_recv, b_send, b_recv, own_sem,
    g_send, g_recv, h_send, h_recv, g_own, f_send, f_recv,
):
    grp, tp, y, c, z, xh = places()
    ring_r, ring_l = 2 * ((z + 1) % 8) + xh, 2 * ((z + 7) % 8) + xh
    dst_grp, dst_tp = z, 2 * (2 * y + xh) + c
    src_grp, src_tp = 2 * (z // 2) + xh, 2 * grp + z % 2
    stays = (dst_grp == grp) & (dst_tp == tp)
    moves = jnp.logical_not(stays)

    barrier = pltpu.get_barrier_semaphore()

    def greet(**where):
        pl.semaphore_signal(barrier, inc=1, device_id=where, device_id_type=MESH)

    @pl.when(moves)
    def _():
        greet(grp=dst_grp, tp=dst_tp)
        greet(grp=src_grp, tp=src_tp)

    greet(tp=ring_r)
    greet(tp=ring_l)
    greet(tp=tp ^ 1)
    greet(grp=grp ^ 1)
    greet(grp=grp ^ 1, tp=tp ^ 1)
    for d in (1, 2, 3):
        greet(grp=2 * ((y + d) % 4) + c)
    pl.semaphore_wait(barrier, jnp.where(moves, 10, 8))

    def rows(ch):
        return pl.ds(128 * ch, 128)

    def perm(ch):
        return remote(
            x_hbm.at[rows(ch)], xs.at[2 * y + xh, rows(ch)], perm_send.at[ch], perm_recv.at[ch], grp=dst_grp, tp=dst_tp
        )

    def perm_local(ch):
        return pltpu.make_async_copy(x_hbm.at[rows(ch)], xs.at[z, rows(ch)], perm_recv.at[ch])

    for ch in (0, 1):
        pl.when(moves)(lambda ch=ch: perm(ch).start())
        pl.when(stays)(lambda ch=ch: perm_local(ch).start())

    w_out = [
        remote(wq_hbm, ws.at[1, :, pl.ds(0, 512)], w_send.at[0], w_recv.at[0], tp=tp ^ 1),
        remote(wkv_hbm, ws.at[1, :, pl.ds(512, 128)], w_send.at[1], w_recv.at[1], tp=tp ^ 1),
    ]
    w_in = [
        pltpu.make_async_copy(wq_hbm, ws.at[0, :, pl.ds(0, 512)], w_local.at[0]),
        pltpu.make_async_copy(wkv_hbm, ws.at[0, :, pl.ds(512, 128)], w_local.at[1]),
    ]
    for copy in w_out + w_in:
        copy.start()
    wo = OutputWeights(
        wo_hbm.at[:, pl.ds(pl.multiple_of(512 * xh, 512), 512)], wo_own, g_send, g_recv, h_send, h_recv, g_own.at[0]
    )
    wo.start()

    def ring(right, k, ch, place):
        ss, rs, to = (r_send, r_recv, ring_r) if right else (l_send, l_recv, ring_l)
        block = xs.at[place, rows(ch)]
        return remote(block, block, ss.at[k - 1, ch], rs.at[k - 1, ch], tp=to)

    sent = []

    def send(copy):
        copy.start()
        sent.append(copy)

    def travels(right, k, ch):
        return k < 4 or (k == 4 and ch == (0 if right else 1))

    for ch in (0, 1):
        pl.when(moves)(lambda ch=ch: remote(
            x_hbm.at[rows(ch)], xs.at[z, rows(ch)], perm_send.at[ch], perm_recv.at[ch], grp=dst_grp, tp=dst_tp
        ).wait_recv())
        pl.when(stays)(lambda ch=ch: perm_local(ch).wait())
        for right in (True, False):
            send(ring(right, 1, ch, z))

    even = z % 2 == 0
    pair = z // 2
    order = [
        pair,
        jnp.where(even, pair + 3, pair + 1) % 4,
        jnp.where(even, pair + 1, pair + 3) % 4,
        (pair + 2) % 4,
    ]

    def product(j, yp, half):
        block = pl.ds(pl.multiple_of(128 * half, 128), 128)
        return dot(xs[2 * yp, block, :], ws[j, :512, :]) + dot(xs[2 * yp + 1, block, :], ws[j, 512:, :])

    def core_copy(j, i):
        return remote(to_core.at[j, i], from_core.at[j, i], c_send.at[j, i], c_recv.at[j, i], grp=grp ^ 1)

    def compute(j, i):
        to_core[j, i] = product(j, order[i], c ^ 1).astype(BF)
        send(core_copy(j, i))
        mine[j, i] = product(j, order[i], c)

    def y_copy(j, i, d):
        return remote(
            to_y.at[j, i], from_y.at[j, d - 1], y_send.at[j, i], y_recv.at[j, d - 1],
            grp=2 * ((y + d) % 4) + c,
        )

    def pass_on(j, i):
        core_copy(j, i).wait_recv()
        total = mine[j, i] + from_core[j, i].astype(F32)
        d = (order[i] - y + 4) % 4

        @pl.when(d == 0)
        def _():
            keep[j] = total

        @pl.when(d != 0)
        def _():
            to_y[j, i] = total.astype(BF)
            y_copy(j, i, d).start()

    for copy in w_in:
        copy.wait()
    for k in (1, 2, 3, 4):
        for ch in (0, 1):
            for right in (True, False):
                if not travels(right, k, ch):
                    continue
                place = (z + 8 - k) % 8 if right else (z + k) % 8
                ring(right, k, ch, place).wait_recv()
                if k < 4 and travels(right, k + 1, ch):
                    send(ring(right, k + 1, ch, place))
        compute(0, k - 1)
        if k > 1:
            pass_on(0, k - 2)
        if k == 2:
            wo.middle()
    pass_on(0, 3)
    for copy in w_out:
        copy.wait_recv()
    far_cols = pl.ds(pl.multiple_of(512 * (xh ^ 1), 512), 512)
    far = remote(wo_hbm.at[:, far_cols], wo_far, f_send.at[0], f_recv.at[0], tp=tp ^ 1)
    far.start()
    for i in range(4):
        compute(1, i)
        if i > 0:
            pass_on(1, i - 1)
    pass_on(1, 3)
    wo.last()

    near = c == xh

    def place_of(cols, half):
        return qkv_out.at[cols, pl.ds(pl.multiple_of(128 * half, 128), 128)]

    for j in (0, 1):
        total = keep[j]
        for d in (1, 2, 3):
            remote(to_y.at[j, 0], from_y.at[j, d - 1], y_send.at[j, 0], y_recv.at[j, d - 1], grp=grp).wait_recv()
            total = total + from_y[j, d - 1].astype(F32)
        final[j] = total.astype(BF)
        spot = place_of(xh ^ j, c)

        @pl.when(near)
        def _():
            pltpu.make_async_copy(final.at[j], spot, own_sem.at[j]).start()

        @pl.when(jnp.logical_not(near))
        def _():
            remote(final.at[j], spot, a_send.at[j], a_recv.at[j], grp=grp ^ 1).start()

        remote(final.at[j], spot, b_send.at[j], b_recv.at[j, c], grp=2 * y + xh, tp=tp ^ 1).start()

    for j in (0, 1):
        spot = place_of(xh ^ j, c)

        @pl.when(near)
        def _():
            pltpu.make_async_copy(final.at[j], spot, own_sem.at[j]).wait()
            remote(final.at[j], place_of(xh ^ j, c ^ 1), a_send.at[j], a_recv.at[j], grp=grp ^ 1).wait_recv()

        @pl.when(jnp.logical_not(near))
        def _():
            remote(final.at[j], spot, a_send.at[j], a_recv.at[j], grp=grp ^ 1).wait_send()
            for half in (0, 1):
                remote(
                    final.at[j], place_of(xh ^ 1 ^ j, half), b_send.at[j], b_recv.at[j, half],
                    grp=2 * y + xh, tp=tp ^ 1,
                ).wait_recv()

        remote(final.at[j], spot, b_send.at[j], b_recv.at[j, c], grp=2 * y + xh, tp=tp ^ 1).wait_send()

    for copy in sent:
        copy.wait_send()
    for copy in w_out:
        copy.wait_send()
    for ch in (0, 1):
        pl.when(moves)(lambda ch=ch: perm(ch).wait_send())
    for j in (0, 1):
        for i in range(4):
            d = (order[i] - y + 4) % 4
            pl.when(d != 0)(lambda j=j, i=i, d=d: y_copy(j, i, d).wait_send())
    wo.finish()
    far.wait()


def project(x, wq, wkv, wo):
    dma = pltpu.SemaphoreType.DMA
    anywhere = pl.BlockSpec(memory_space=pl.ANY)
    return pl.pallas_call(
        project_kernel,
        out_shape=(
            jax.ShapeDtypeStruct((2, 256, 640), BF),
            jax.ShapeDtypeStruct((8, 512, 512), BF),
            jax.ShapeDtypeStruct((512, 512), BF),
        ),
        in_specs=[anywhere] * 4,
        out_specs=(anywhere,) * 3,
        scratch_shapes=[
            pltpu.VMEM((8, 256, 512), BF),
            pltpu.VMEM((2, 1024, 640), BF),
            pltpu.VMEM((2, 4, 128, 640), F32),
            pltpu.VMEM((2, 128, 640), F32),
            pltpu.VMEM((2, 4, 128, 640), BF),
            pltpu.VMEM((2, 4, 128, 640), BF),
            pltpu.VMEM((2, 4, 128, 640), BF),
            pltpu.VMEM((2, 3, 128, 640), BF),
            pltpu.VMEM((2, 128, 640), BF),
            dma((2,)), dma((2,)), dma((4, 2)), dma((4, 2)), dma((4, 2)), dma((4, 2)), dma((2,)), dma((2,)), dma((2,)),
            dma((2, 4)), dma((2, 4)), dma((2, 4)), dma((2, 3)), dma((2,)), dma((2,)), dma((2,)), dma((2, 2)), dma((2,)),
            dma((4,)), dma((4,)), dma((4,)), dma((4,)), dma((1,)), dma((1,)), dma((1,)),
        ],
        compiler_params=pltpu.CompilerParams(
            collective_id=0, has_side_effects=True, vmem_limit_bytes=40 * MIB
        ),
        name="project",
    )(x, wq, wkv, wo)


def attend_kernel(q_ref, kv_ref, len_ref, out_ref, lse_ref, q_rows):
    step = pl.program_id(0)
    leader = lax.axis_index("tp") % 2 == 0
    scale = HD ** -0.5
    lane = lax.broadcasted_iota(jnp.int32, (1, 128), 1)
    pos = lax.broadcasted_iota(jnp.int32, (256, 128), 0)
    lane_roll, lane_step = lane // 32, lane % 32 // 8
    new_row = lax.broadcasted_iota(jnp.int32, (16, 128), 0)
    causal = (new_row // 4 == lane_roll) & (new_row % 4 <= lane_step) & leader
    for group in range(2):
        tokens = pl.ds(16 * group, 16)
        for part in (0, 1):
            vals = q_ref[part, tokens, :].astype(F32)
            for head in range(4):
                q_rows[pl.ds(4 * part + head, 16, stride=8), :] = vals[:, 128 * head:128 * head + 128]
        new_key = q_ref[0, tokens, 512:]
        new_val = q_ref[1, tokens, 512:]
        q_t = q_rows[...].T.astype(BF)
        cached = None
        for i in range(4):
            one = dot(kv_ref[4 * group + i, :, :128], q_t)
            cached = one if cached is None else jnp.where(lane_roll == i, one, cached)
        visible = pos < len_ref[0, group:group + 1, :]
        cached = jnp.where(visible, cached * scale, -1e30)
        fresh = jnp.where(causal, dot(new_key, q_t) * scale, -1e30)
        peak = jnp.maximum(jnp.max(cached, axis=0, keepdims=True), jnp.max(fresh, axis=0, keepdims=True))
        cached = jnp.where(visible, jnp.exp(cached - peak), 0.0)
        fresh = jnp.where(causal, jnp.exp(fresh - peak), 0.0)
        total = jnp.sum(cached, axis=0, keepdims=True) + jnp.sum(fresh, axis=0, keepdims=True)
        lse_ref[0, group:group + 1, :] = jnp.where(total > 0.0, peak + jnp.log(jnp.maximum(total, 1e-30)), -1e30)
        inverse = jnp.where(total > 0.0, 1.0 / jnp.maximum(total, 1e-30), 0.0)
        weights = (cached * inverse).T.astype(BF)
        fresh_w = jnp.concatenate([fresh * inverse, jnp.zeros((112, 128), F32)], axis=0).T.astype(BF)
        new_pad = jnp.concatenate([new_val, jnp.zeros((112, 128), BF)], axis=0)
        added = dot(fresh_w, new_pad)
        for i in range(4):
            block = slice(32 * i, 32 * i + 32)
            got = dot(weights[block], kv_ref[4 * group + i, :, 128:]) + added[block]
            out_ref[pl.ds(128 * group + 32 * i, 32), :] = got.astype(BF)


def attend(qkv, cache, spans):
    return pl.pallas_call(
        attend_kernel,
        grid=(8,),
        out_shape=(jax.ShapeDtypeStruct((2048, 128), BF), jax.ShapeDtypeStruct((8, 2, 128), F32)),
        in_specs=[
            pl.BlockSpec((2, 32, 640), lambda i: (0, i, 0)),
            pl.BlockSpec((8, 256, 256), lambda i: (i, 0, 0)),
            pl.BlockSpec((1, 2, 128), lambda i: (i, 0, 0)),
        ],
        out_specs=(
            pl.BlockSpec((256, 128), lambda i: (i, 0)),
            pl.BlockSpec((1, 2, 128), lambda i: (i, 0, 0)),
        ),
        scratch_shapes=[pltpu.VMEM((128, 128), F32)],
        compiler_params=pltpu.CompilerParams(vmem_limit_bytes=16 * MIB),
        name="attend",
    )(qkv, cache, spans)


def finish_kernel(
    o_ref, lse_ref, wo_own_hbm, wo_far_hbm, head_ref, hidden_out, gap_out,
    o_got, lse_got, near_w, far_w, merged, ctx, outgo, income, gap_own, gap_x, gap_z,
    o_send, o_recv, s_send, s_recv, near_sem,
    g_send, g_recv, h_send, h_recv, g_own,
    ring_send, ring_recv, gx_send, gx_recv, gz_send, gz_recv,
):
    grp, tp, y, c, z, xh = places()
    sec = lax.axis_index("sec")
    barrier = pltpu.get_barrier_semaphore()

    def greet(**where):
        pl.semaphore_signal(barrier, inc=1, device_id=where, device_id_type=MESH)

    greet(tp=tp ^ 1)
    greet(sec=sec ^ 1)
    greet(tp=tp ^ 1, sec=sec ^ 1)
    greet(grp=grp ^ 1)
    for d in (1, 2, 3):
        greet(grp=2 * ((y + d) % 4) + c)
    for d in range(1, 8):
        greet(tp=2 * ((z + d) % 8) + xh)
    pl.semaphore_wait(barrier, 14)

    stats = remote(lse_ref, lse_got, s_send.at[0], s_recv.at[0], tp=tp ^ 1)
    stats.start()
    parts = []
    for n in range(4):
        block = pl.ds(512 * n, 512)
        parts.append(remote(o_ref.at[block], o_got.at[block], o_send.at[n], o_recv.at[n], tp=tp ^ 1))
        parts[-1].start()
    near = pltpu.make_async_copy(wo_own_hbm, near_w, near_sem.at[0])
    near.start()
    wo = OutputWeights(wo_far_hbm, far_w, g_send, g_recv, h_send, h_recv, g_own.at[0])
    wo.start()

    stats.wait_recv()
    for n in range(4):
        parts[n].wait_recv()
        for m in range(4 * n, 4 * n + 4):
            factor = 1.0 / (1.0 + jnp.exp(lse_got[m // 2, m % 2:m % 2 + 1, :] - lse_ref[m // 2, m % 2:m % 2 + 1, :]))
            factor = jnp.broadcast_to(factor, (128, 128)).T
            block = slice(128 * m, 128 * m + 128)
            own = o_ref[block, :].astype(F32)
            got = o_got[block, :].astype(F32)
            merged[block, :] = own * factor + got * (1.0 - factor)
        if n == 1:
            wo.middle()
    for part in (0, 1):
        for head in range(4):
            ctx[part, :, pl.ds(128 * head, 128)] = merged[pl.ds(4 * part + head, 256, stride=8), :].astype(BF)
    near.wait()
    wo.last()
    wo.finish()

    def block(place, ch):
        return dot(ctx[xh, 128 * ch:128 * ch + 128, :], near_w[place]) + dot(
            ctx[xh ^ 1, 128 * ch:128 * ch + 128, :], far_w[place]
        )

    def slot(right, ch):
        return 2 * ch + (0 if right else 1)

    def ring(right, ch, k):
        s = slot(right, ch)
        to = 2 * ((z + (1 if right else 7)) % 8) + xh
        return remote(outgo.at[s, k - 1], income.at[s, k - 1], ring_send.at[s, k - 1], ring_recv.at[s, k - 1], tp=to)

    sent = []

    def longest(right, ch):
        return 4 if ch == (0 if right else 1) else 3

    for turn in range(4):
        for right, ch in ((True, 0), (False, 1), (True, 1), (False, 0)):
            k = longest(right, ch) - turn
            if k < 1:
                continue
            place = (z + k) % 8 if right else (z + 8 - k) % 8
            total = block(place, ch)
            if turn > 0:
                ring(right, ch, k + 1).wait_recv()
                total = total + income[slot(right, ch), k].astype(F32)
            outgo[slot(right, ch), k - 1] = total.astype(BF)
            copy = ring(right, ch, k)
            copy.start()
            sent.append(copy)

    value = head_ref[...]
    first = value.astype(BF)
    rest = value - first.astype(F32)
    second = rest.astype(BF)
    third = (rest - second.astype(F32)).astype(BF)
    which = lax.broadcasted_iota(jnp.int32, (16, 512), 0)
    triple = jnp.where(
        which == 0, first.astype(F32),
        jnp.where(which == 1, second.astype(F32), jnp.where(which == 2, third.astype(F32), 0.0)),
    ).astype(BF)
    gaps = []
    for ch in (0, 1):
        total = block(z, ch)
        for right in (True, False):
            ring(right, ch, 1).wait_recv()
            total = total + income[slot(right, ch), 0].astype(F32)
        result = total.astype(BF)
        hidden_out[128 * ch:128 * ch + 128, :] = result
        gaps.append(jnp.sum(dot_nt(triple, result), axis=0, keepdims=True))
    gap = jnp.concatenate(gaps, axis=1)
    gap = jnp.where(sec == 0, gap, -gap)
    own_x = 2 * xh + sec
    gap_own[...] = jnp.broadcast_to(gap, (8, 256))

    def gap_far(d):
        return remote(
            gap_own, gap_x.at[own_x], gx_send.at[d - 1], gx_recv.at[d - 1], tp=tp ^ (d // 2), sec=sec ^ (d % 2)
        )

    for d in (1, 2, 3):
        gap_far(d).start()
    gap_x[own_x] = gap_own[...]
    for d in (1, 2, 3):
        gap_far(d).wait_recv()
    gap_z[z] = gap_x[0] + gap_x[1] + gap_x[2] + gap_x[3]

    def gap_ring(d):
        return remote(
            gap_z.at[z], gap_z.at[z], gz_send.at[d - 1], gz_recv.at[d - 1], tp=2 * ((z + d) % 8) + xh
        )

    for d in range(1, 8):
        gap_ring(d).start()
    for d in range(1, 8):
        gap_ring(d).wait_recv()
    total = gap_z[0]
    for n in range(1, 8):
        total = total + gap_z[n]
    gap_out[...] = total

    for d in (1, 2, 3):
        gap_far(d).wait_send()
    for d in range(1, 8):
        gap_ring(d).wait_send()
    for copy in sent:
        copy.wait_send()
    stats.wait_send()
    for copy in parts:
        copy.wait_send()


def finish(o, lse, wo_own, wo_far, value_head):
    dma = pltpu.SemaphoreType.DMA
    anywhere = pl.BlockSpec(memory_space=pl.ANY)
    vmem = pl.BlockSpec(memory_space=pltpu.VMEM)
    return pl.pallas_call(
        finish_kernel,
        out_shape=(jax.ShapeDtypeStruct((256, 512), BF), jax.ShapeDtypeStruct((8, 256), F32)),
        in_specs=[vmem, vmem, anywhere, anywhere, vmem],
        out_specs=(vmem, vmem),
        scratch_shapes=[
            pltpu.VMEM((2048, 128), BF),
            pltpu.VMEM((8, 2, 128), F32),
            pltpu.VMEM((8, 512, 512), BF),
            pltpu.VMEM((8, 512, 512), BF),
            pltpu.VMEM((2048, 128), F32),
            pltpu.VMEM((2, 256, 512), BF),
            pltpu.VMEM((4, 4, 128, 512), BF),
            pltpu.VMEM((4, 4, 128, 512), BF),
            pltpu.VMEM((8, 256), F32),
            pltpu.VMEM((4, 8, 256), F32),
            pltpu.VMEM((8, 8, 256), F32),
            dma((4,)), dma((4,)), dma((1,)), dma((1,)), dma((1,)),
            dma((4,)), dma((4,)), dma((4,)), dma((4,)), dma((1,)),
            dma((4, 4)), dma((4, 4)), dma((3,)), dma((3,)), dma((7,)), dma((7,)),
        ],
        compiler_params=pltpu.CompilerParams(
            collective_id=1, has_side_effects=True, vmem_limit_bytes=40 * MIB
        ),
        name="finish",
    )(o, lse, wo_own, wo_far, value_head)


def local(layer_in, q_weight, kv_weight, o_weight, kv_cache, cache_lengths, value_head):
    xh = lax.axis_index("tp") % 2
    x = layer_in[0].reshape(256, 512)
    qkv, wo_own, wo_far = project(x, q_weight[0], kv_weight[0], o_weight[0])
    spans = jnp.repeat(cache_lengths - xh * 256, 32).reshape(8, 2, 128)
    o, lse = attend(qkv, kv_cache[0], spans)
    hidden, gap = finish(o, lse, wo_own, wo_far, value_head.reshape(1, 512))
    hidden_out = hidden.reshape(1, 64, 4, 512)
    own_gap = lax.dynamic_slice_in_dim(gap[0].reshape(64, 4), 2 * lax.axis_index("sec"), 2, 1)
    return hidden_out, own_gap


def solution(mesh):
    placed = (
        P("sec", "grp", None, "tp"),
        P("sec", "grp", "tp"),
        P("sec", "grp", "tp"),
        P("sec", "tp", "grp"),
        P("sec", "grp", "tp", None),
        P("grp"),
        P("tp"),
    )
    return jax.shard_map(
        local,
        mesh=mesh,
        in_specs=placed,
        out_specs=(P("sec", "grp", None, "tp"), P("grp", "sec")),
        check_vma=False,
    )
```

```python
import functools

import jax
import jax.numpy as jnp
from jax import lax
from jax.experimental import pallas as pl
from jax.experimental.pallas import tpu as pltpu
from jax.sharding import PartitionSpec as P

HD = 128
CACHE = 512
MESH = pl.DeviceIdType.MESH
BF = jnp.bfloat16
F32 = jnp.float32
MIB = 1024 * 1024


def dot(a, b):
    return jnp.dot(a, b, preferred_element_type=F32)


def dot_nt(a, b):
    return lax.dot_general(a, b, (((1,), (1,)), ((), ())), preferred_element_type=F32)


def remote(src, dst, send, recv, **where):
    return pltpu.make_async_remote_copy(
        src_ref=src, dst_ref=dst, send_sem=send, recv_sem=recv, device_id=where, device_id_type=MESH
    )


def places():
    grp, tp = lax.axis_index("grp"), lax.axis_index("tp")
    return grp, tp, grp // 2, grp % 2, tp // 2, tp % 2


class OutputWeights:
    def __init__(self, src, full, y_send, y_recv, c_send, c_recv, own_sem):
        grp, tp, y, c, z, xh = places()
        self.grp, self.c, self.y = grp, c, y
        self.right, self.left = 2 * ((y + 1) % 4) + c, 2 * ((y + 3) % 4) + c
        self.src, self.full = src, full
        self.y_send, self.y_recv, self.c_send, self.c_recv, self.own_sem = y_send, y_recv, c_send, c_recv, own_sem

    def to_core(self, slot, src, place):
        return remote(src, self.full.at[place], self.c_send.at[slot], self.c_recv.at[slot], grp=self.grp ^ 1)

    def from_core(self, slot, place):
        return remote(
            self.full.at[place], self.full.at[place ^ 1], self.c_send.at[slot], self.c_recv.at[slot], grp=self.grp ^ 1
        )

    def one(self, which, place, src=None):
        to = self.right if which == 0 else self.left
        return remote(
            self.full.at[place] if src is None else src, self.full.at[place],
            self.y_send.at[which], self.y_recv.at[which], grp=to,
        )

    def half(self, which, place):
        to = self.right if which == 0 else self.left
        rows = pl.ds(256 * which, 256)
        return remote(
            self.full.at[place, rows], self.full.at[place, rows],
            self.y_send.at[2 + which], self.y_recv.at[2 + which], grp=to,
        )

    def start(self):
        self.own = pltpu.make_async_copy(self.src, self.full.at[self.grp], self.own_sem)
        self.own.start()
        self.sent = [self.one(0, self.grp, self.src), self.one(1, self.grp, self.src), self.to_core(0, self.src, self.grp)]
        for copy in self.sent:
            copy.start()

    def middle(self):
        for which, place in ((0, self.left), (1, self.right)):
            self.one(which, place).wait_recv()
            ahead = self.half(which, place)
            ahead.start()
            over = self.to_core(1 + which, self.full.at[place], place)
            over.start()
            self.sent += [ahead, over]

    def last(self):
        far = 2 * ((self.y + 2) % 4) + self.c
        for which in (0, 1):
            self.half(which, far).wait_recv()
        over = self.to_core(3, self.full.at[far], far)
        over.start()
        self.sent.append(over)

    def finish(self):
        self.own.wait()
        for copy in self.sent:
            copy.wait_send()
        for slot in range(4):
            self.from_core(slot, self.grp).wait_recv()


def project_kernel(
    x_hbm, wq_hbm, wkv_hbm, wo_hbm, qkv_out, wo_own, wo_far,
    swapped, xs, ws, mine, keep, to_core, from_core, to_y, from_y, final,
    perm_send, perm_recv, r_send, r_recv, l_send, l_recv, w_local, w_send, w_recv,
    c_send, c_recv, y_send, y_recv, a_send, a_recv, b_send, b_recv, own_sem,
    g_send, g_recv, h_send, h_recv, g_own, f_send, f_recv, i_send, i_recv, j_send, j_recv, i_own,
):
    grp, tp, y, c, z, xh = places()
    ring_r, ring_l = 2 * ((z + 1) % 8) + xh, 2 * ((z + 7) % 8) + xh
    dst_grp, dst_tp = z, 2 * (2 * y + xh) + c
    src_grp, src_tp = 2 * (z // 2) + xh, 2 * grp + z % 2
    stays = (dst_grp == grp) & (dst_tp == tp)
    moves = jnp.logical_not(stays)

    barrier = pltpu.get_barrier_semaphore()

    def greet(**where):
        pl.semaphore_signal(barrier, inc=1, device_id=where, device_id_type=MESH)

    @pl.when(moves)
    def _():
        greet(grp=dst_grp, tp=dst_tp)
        greet(grp=src_grp, tp=src_tp)

    greet(tp=ring_r)
    greet(tp=ring_l)
    greet(tp=tp ^ 1)
    greet(grp=grp ^ 1)
    greet(grp=grp ^ 1, tp=tp ^ 1)
    for d in (1, 2, 3):
        greet(grp=2 * ((y + d) % 4) + c)
    pl.semaphore_wait(barrier, jnp.where(moves, 10, 8))

    def rows(ch):
        return pl.ds(128 * ch, 128)

    def perm(ch):
        return remote(
            x_hbm.at[rows(ch)], xs.at[2 * y + xh, rows(ch)], perm_send.at[ch], perm_recv.at[ch], grp=dst_grp, tp=dst_tp
        )

    def perm_local(ch):
        return pltpu.make_async_copy(x_hbm.at[rows(ch)], xs.at[z, rows(ch)], perm_recv.at[ch])

    for ch in (0, 1):
        pl.when(moves)(lambda ch=ch: perm(ch).start())
        pl.when(stays)(lambda ch=ch: perm_local(ch).start())

    w_out = [
        remote(wq_hbm, ws.at[1, :, pl.ds(0, 512)], w_send.at[0], w_recv.at[0], tp=tp ^ 1),
        remote(wkv_hbm, ws.at[1, :, pl.ds(512, 128)], w_send.at[1], w_recv.at[1], tp=tp ^ 1),
    ]
    w_in = [
        pltpu.make_async_copy(wq_hbm, ws.at[0, :, pl.ds(0, 512)], w_local.at[0]),
        pltpu.make_async_copy(wkv_hbm, ws.at[0, :, pl.ds(512, 128)], w_local.at[1]),
    ]
    far_cols = pl.ds(pl.multiple_of(512 * (xh ^ 1), 512), 512)
    far = remote(wo_hbm.at[:, far_cols], swapped, f_send.at[0], f_recv.at[0], tp=tp ^ 1)
    far.start()
    for copy in w_out + w_in:
        copy.start()
    wo = OutputWeights(
        wo_hbm.at[:, pl.ds(pl.multiple_of(512 * xh, 512), 512)], wo_own, g_send, g_recv, h_send, h_recv, g_own.at[0]
    )
    wo.start()
    wo2 = OutputWeights(swapped, wo_far, i_send, i_recv, j_send, j_recv, i_own.at[0])

    def ring(right, k, ch, place):
        ss, rs, to = (r_send, r_recv, ring_r) if right else (l_send, l_recv, ring_l)
        block = xs.at[place, rows(ch)]
        return remote(block, block, ss.at[k - 1, ch], rs.at[k - 1, ch], tp=to)

    sent = []

    def send(copy):
        copy.start()
        sent.append(copy)

    def travels(right, k, ch):
        return k < 4 or (k == 4 and ch == (0 if right else 1))

    for ch in (0, 1):
        pl.when(moves)(lambda ch=ch: remote(
            x_hbm.at[rows(ch)], xs.at[z, rows(ch)], perm_send.at[ch], perm_recv.at[ch], grp=dst_grp, tp=dst_tp
        ).wait_recv())
        pl.when(stays)(lambda ch=ch: perm_local(ch).wait())
        for right in (True, False):
            send(ring(right, 1, ch, z))

    even = z % 2 == 0
    pair = z // 2
    order = [
        pair,
        jnp.where(even, pair + 3, pair + 1) % 4,
        jnp.where(even, pair + 1, pair + 3) % 4,
        (pair + 2) % 4,
    ]

    def product(j, yp, half):
        block = pl.ds(pl.multiple_of(128 * half, 128), 128)
        return dot(xs[2 * yp, block, :], ws[j, :512, :]) + dot(xs[2 * yp + 1, block, :], ws[j, 512:, :])

    def core_copy(j, i):
        return remote(to_core.at[j, i], from_core.at[j, i], c_send.at[j, i], c_recv.at[j, i], grp=grp ^ 1)

    def compute(j, i):
        to_core[j, i] = product(j, order[i], c ^ 1).astype(BF)
        send(core_copy(j, i))
        mine[j, i] = product(j, order[i], c)

    def y_copy(j, i, d):
        return remote(
            to_y.at[j, i], from_y.at[j, d - 1], y_send.at[j, i], y_recv.at[j, d - 1],
            grp=2 * ((y + d) % 4) + c,
        )

    def pass_on(j, i):
        core_copy(j, i).wait_recv()
        total = mine[j, i] + from_core[j, i].astype(F32)
        d = (order[i] - y + 4) % 4

        @pl.when(d == 0)
        def _():
            keep[j] = total

        @pl.when(d != 0)
        def _():
            to_y[j, i] = total.astype(BF)
            y_copy(j, i, d).start()

    for copy in w_in:
        copy.wait()
    for k in (1, 2, 3, 4):
        for ch in (0, 1):
            for right in (True, False):
                if not travels(right, k, ch):
                    continue
                place = (z + 8 - k) % 8 if right else (z + k) % 8
                ring(right, k, ch, place).wait_recv()
                if k < 4 and travels(right, k + 1, ch):
                    send(ring(right, k + 1, ch, place))
        if k < 4:
            compute(0, k - 1)
        if k == 1:
            far.wait_recv()
            wo2.start()
        if k == 2:
            pass_on(0, 0)
            wo.middle()
        if k == 3:
            pass_on(0, 1)
            for copy in w_out:
                copy.wait_recv()
            compute(1, 0)
            compute(1, 1)
            pass_on(0, 2)
            compute(1, 2)
            wo.last()
            wo2.middle()
            pass_on(1, 0)
            pass_on(1, 1)
    compute(0, 3)
    compute(1, 3)
    pass_on(1, 2)
    pass_on(0, 3)
    pass_on(1, 3)
    wo2.last()

    near = c == xh

    def place_of(cols, half):
        return qkv_out.at[cols, pl.ds(pl.multiple_of(128 * half, 128), 128)]

    for j in (0, 1):
        total = keep[j]
        for d in (1, 2, 3):
            remote(to_y.at[j, 0], from_y.at[j, d - 1], y_send.at[j, 0], y_recv.at[j, d - 1], grp=grp).wait_recv()
            total = total + from_y[j, d - 1].astype(F32)
        final[j] = total.astype(BF)
        spot = place_of(xh ^ j, c)

        @pl.when(near)
        def _():
            pltpu.make_async_copy(final.at[j], spot, own_sem.at[j]).start()

        @pl.when(jnp.logical_not(near))
        def _():
            remote(final.at[j], spot, a_send.at[j], a_recv.at[j], grp=grp ^ 1).start()

        remote(final.at[j], spot, b_send.at[j], b_recv.at[j, c], grp=2 * y + xh, tp=tp ^ 1).start()

    for j in (0, 1):
        spot = place_of(xh ^ j, c)

        @pl.when(near)
        def _():
            pltpu.make_async_copy(final.at[j], spot, own_sem.at[j]).wait()
            remote(final.at[j], place_of(xh ^ j, c ^ 1), a_send.at[j], a_recv.at[j], grp=grp ^ 1).wait_recv()

        @pl.when(jnp.logical_not(near))
        def _():
            remote(final.at[j], spot, a_send.at[j], a_recv.at[j], grp=grp ^ 1).wait_send()
            for half in (0, 1):
                remote(
                    final.at[j], place_of(xh ^ 1 ^ j, half), b_send.at[j], b_recv.at[j, half],
                    grp=2 * y + xh, tp=tp ^ 1,
                ).wait_recv()

        remote(final.at[j], spot, b_send.at[j], b_recv.at[j, c], grp=2 * y + xh, tp=tp ^ 1).wait_send()

    for copy in sent:
        copy.wait_send()
    for copy in w_out:
        copy.wait_send()
    for ch in (0, 1):
        pl.when(moves)(lambda ch=ch: perm(ch).wait_send())
    for j in (0, 1):
        for i in range(4):
            d = (order[i] - y + 4) % 4
            pl.when(d != 0)(lambda j=j, i=i, d=d: y_copy(j, i, d).wait_send())
    wo.finish()
    wo2.finish()
    far.wait_send()


def project(x, wq, wkv, wo):
    dma = pltpu.SemaphoreType.DMA
    anywhere = pl.BlockSpec(memory_space=pl.ANY)
    return pl.pallas_call(
        project_kernel,
        out_shape=(
            jax.ShapeDtypeStruct((2, 256, 640), BF),
            jax.ShapeDtypeStruct((8, 512, 512), BF),
            jax.ShapeDtypeStruct((8, 512, 512), BF),
        ),
        in_specs=[anywhere] * 4,
        out_specs=(anywhere,) * 3,
        scratch_shapes=[
            pltpu.VMEM((512, 512), BF),
            pltpu.VMEM((8, 256, 512), BF),
            pltpu.VMEM((2, 1024, 640), BF),
            pltpu.VMEM((2, 4, 128, 640), F32),
            pltpu.VMEM((2, 128, 640), F32),
            pltpu.VMEM((2, 4, 128, 640), BF),
            pltpu.VMEM((2, 4, 128, 640), BF),
            pltpu.VMEM((2, 4, 128, 640), BF),
            pltpu.VMEM((2, 3, 128, 640), BF),
            pltpu.VMEM((2, 128, 640), BF),
            dma((2,)), dma((2,)), dma((4, 2)), dma((4, 2)), dma((4, 2)), dma((4, 2)), dma((2,)), dma((2,)), dma((2,)),
            dma((2, 4)), dma((2, 4)), dma((2, 4)), dma((2, 3)), dma((2,)), dma((2,)), dma((2,)), dma((2, 2)), dma((2,)),
            dma((4,)), dma((4,)), dma((4,)), dma((4,)), dma((1,)), dma((1,)), dma((1,)),
            dma((4,)), dma((4,)), dma((4,)), dma((4,)), dma((1,)),
        ],
        compiler_params=pltpu.CompilerParams(
            collective_id=0, has_side_effects=True, vmem_limit_bytes=58 * MIB
        ),
        name="project",
    )(x, wq, wkv, wo)


def attend_kernel(q_ref, kv_ref, len_ref, out_ref, lse_ref, q_rows):
    step = pl.program_id(0)
    leader = lax.axis_index("tp") % 2 == 0
    scale = HD ** -0.5
    lane = lax.broadcasted_iota(jnp.int32, (1, 128), 1)
    pos = lax.broadcasted_iota(jnp.int32, (256, 128), 0)
    lane_roll, lane_step = lane // 32, lane % 32 // 8
    new_row = lax.broadcasted_iota(jnp.int32, (16, 128), 0)
    causal = (new_row // 4 == lane_roll) & (new_row % 4 <= lane_step) & leader
    for group in range(2):
        tokens = pl.ds(16 * group, 16)
        for part in (0, 1):
            vals = q_ref[part, tokens, :].astype(F32)
            for head in range(4):
                q_rows[pl.ds(4 * part + head, 16, stride=8), :] = vals[:, 128 * head:128 * head + 128]
        new_key = q_ref[0, tokens, 512:]
        new_val = q_ref[1, tokens, 512:]
        q_t = q_rows[...].T.astype(BF)
        cached = None
        for i in range(4):
            one = dot(kv_ref[4 * group + i, :, :128], q_t)
            cached = one if cached is None else jnp.where(lane_roll == i, one, cached)
        visible = pos < len_ref[0, group:group + 1, :]
        cached = jnp.where(visible, cached * scale, -1e30)
        fresh = jnp.where(causal, dot(new_key, q_t) * scale, -1e30)
        peak = jnp.maximum(jnp.max(cached, axis=0, keepdims=True), jnp.max(fresh, axis=0, keepdims=True))
        cached = jnp.where(visible, jnp.exp(cached - peak), 0.0)
        fresh = jnp.where(causal, jnp.exp(fresh - peak), 0.0)
        total = jnp.sum(cached, axis=0, keepdims=True) + jnp.sum(fresh, axis=0, keepdims=True)
        lse_ref[0, group:group + 1, :] = jnp.where(total > 0.0, peak + jnp.log(jnp.maximum(total, 1e-30)), -1e30)
        inverse = jnp.where(total > 0.0, 1.0 / jnp.maximum(total, 1e-30), 0.0)
        weights = (cached * inverse).T.astype(BF)
        fresh_w = jnp.concatenate([fresh * inverse, jnp.zeros((112, 128), F32)], axis=0).T.astype(BF)
        new_pad = jnp.concatenate([new_val, jnp.zeros((112, 128), BF)], axis=0)
        added = dot(fresh_w, new_pad)
        for i in range(4):
            block = slice(32 * i, 32 * i + 32)
            got = dot(weights[block], kv_ref[4 * group + i, :, 128:]) + added[block]
            out_ref[pl.ds(128 * group + 32 * i, 32), :] = got.astype(BF)


def attend(qkv, cache, spans):
    return pl.pallas_call(
        attend_kernel,
        grid=(8,),
        out_shape=(jax.ShapeDtypeStruct((2048, 128), BF), jax.ShapeDtypeStruct((8, 2, 128), F32)),
        in_specs=[
            pl.BlockSpec((2, 32, 640), lambda i: (0, i, 0)),
            pl.BlockSpec((8, 256, 256), lambda i: (i, 0, 0)),
            pl.BlockSpec((1, 2, 128), lambda i: (i, 0, 0)),
        ],
        out_specs=(
            pl.BlockSpec((256, 128), lambda i: (i, 0)),
            pl.BlockSpec((1, 2, 128), lambda i: (i, 0, 0)),
        ),
        scratch_shapes=[pltpu.VMEM((128, 128), F32)],
        compiler_params=pltpu.CompilerParams(vmem_limit_bytes=58 * MIB),
        name="attend",
    )(qkv, cache, spans)


def finish_kernel(
    o_ref, lse_ref, wo_own_hbm, wo_far_hbm, head_ref, hidden_out, gap_out,
    o_got, lse_got, near_w, far_w, merged, ctx, outgo, income, gap_own, gap_x, gap_z,
    o_send, o_recv, s_send, s_recv, near_sem,
    ring_send, ring_recv, gx_send, gx_recv, gz_send, gz_recv,
):
    grp, tp, y, c, z, xh = places()
    sec = lax.axis_index("sec")
    barrier = pltpu.get_barrier_semaphore()

    def greet(**where):
        pl.semaphore_signal(barrier, inc=1, device_id=where, device_id_type=MESH)

    greet(tp=tp ^ 1)
    greet(sec=sec ^ 1)
    greet(tp=tp ^ 1, sec=sec ^ 1)
    for d in range(1, 8):
        greet(tp=2 * ((z + d) % 8) + xh)
    pl.semaphore_wait(barrier, 10)

    stats = remote(lse_ref, lse_got, s_send.at[0], s_recv.at[0], tp=tp ^ 1)
    stats.start()
    parts = []
    for n in range(4):
        block = pl.ds(512 * n, 512)
        parts.append(remote(o_ref.at[block], o_got.at[block], o_send.at[n], o_recv.at[n], tp=tp ^ 1))
        parts[-1].start()
    near = pltpu.make_async_copy(wo_own_hbm, near_w, near_sem.at[0])
    near.start()
    other = pltpu.make_async_copy(wo_far_hbm, far_w, near_sem.at[1])
    other.start()

    stats.wait_recv()
    for n in range(4):
        parts[n].wait_recv()
        for m in range(4 * n, 4 * n + 4):
            factor = 1.0 / (1.0 + jnp.exp(lse_got[m // 2, m % 2:m % 2 + 1, :] - lse_ref[m // 2, m % 2:m % 2 + 1, :]))
            factor = jnp.broadcast_to(factor, (128, 128)).T
            block = slice(128 * m, 128 * m + 128)
            own = o_ref[block, :].astype(F32)
            got = o_got[block, :].astype(F32)
            merged[block, :] = own * factor + got * (1.0 - factor)
    for part in (0, 1):
        for head in range(4):
            ctx[part, :, pl.ds(128 * head, 128)] = merged[pl.ds(4 * part + head, 256, stride=8), :].astype(BF)
    near.wait()
    other.wait()

    def block(place, ch):
        return dot(ctx[xh, 128 * ch:128 * ch + 128, :], near_w[place]) + dot(
            ctx[xh ^ 1, 128 * ch:128 * ch + 128, :], far_w[place]
        )

    def slot(right, ch):
        return 2 * ch + (0 if right else 1)

    def ring(right, ch, k):
        s = slot(right, ch)
        to = 2 * ((z + (1 if right else 7)) % 8) + xh
        return remote(outgo.at[s, k - 1], income.at[s, k - 1], ring_send.at[s, k - 1], ring_recv.at[s, k - 1], tp=to)

    sent = []

    def longest(right, ch):
        return 4 if ch == (0 if right else 1) else 3

    for turn in range(4):
        for right, ch in ((True, 0), (False, 1), (True, 1), (False, 0)):
            k = longest(right, ch) - turn
            if k < 1:
                continue
            place = (z + k) % 8 if right else (z + 8 - k) % 8
            total = block(place, ch)
            if turn > 0:
                ring(right, ch, k + 1).wait_recv()
                total = total + income[slot(right, ch), k].astype(F32)
            outgo[slot(right, ch), k - 1] = total.astype(BF)
            copy = ring(right, ch, k)
            copy.start()
            sent.append(copy)

    value = head_ref[...]
    first = value.astype(BF)
    rest = value - first.astype(F32)
    second = rest.astype(BF)
    third = (rest - second.astype(F32)).astype(BF)
    which = lax.broadcasted_iota(jnp.int32, (16, 512), 0)
    triple = jnp.where(
        which == 0, first.astype(F32),
        jnp.where(which == 1, second.astype(F32), jnp.where(which == 2, third.astype(F32), 0.0)),
    ).astype(BF)
    gaps = []
    for ch in (0, 1):
        total = block(z, ch)
        for right in (True, False):
            ring(right, ch, 1).wait_recv()
            total = total + income[slot(right, ch), 0].astype(F32)
        result = total.astype(BF)
        hidden_out[128 * ch:128 * ch + 128, :] = result
        gaps.append(jnp.sum(dot_nt(triple, result), axis=0, keepdims=True))
    gap = jnp.concatenate(gaps, axis=1)
    gap = jnp.where(sec == 0, gap, -gap)
    own_x = 2 * xh + sec
    gap_own[...] = jnp.broadcast_to(gap, (8, 256))

    def gap_far(d):
        return remote(
            gap_own, gap_x.at[own_x], gx_send.at[d - 1], gx_recv.at[d - 1], tp=tp ^ (d // 2), sec=sec ^ (d % 2)
        )

    for d in (1, 2, 3):
        gap_far(d).start()
    gap_x[own_x] = gap_own[...]
    for d in (1, 2, 3):
        gap_far(d).wait_recv()
    gap_z[z] = gap_x[0] + gap_x[1] + gap_x[2] + gap_x[3]

    def gap_ring(d):
        return remote(
            gap_z.at[z], gap_z.at[z], gz_send.at[d - 1], gz_recv.at[d - 1], tp=2 * ((z + d) % 8) + xh
        )

    for d in range(1, 8):
        gap_ring(d).start()
    for d in range(1, 8):
        gap_ring(d).wait_recv()
    total = gap_z[0]
    for n in range(1, 8):
        total = total + gap_z[n]
    gap_out[...] = total

    for d in (1, 2, 3):
        gap_far(d).wait_send()
    for d in range(1, 8):
        gap_ring(d).wait_send()
    for copy in sent:
        copy.wait_send()
    stats.wait_send()
    for copy in parts:
        copy.wait_send()


def finish(o, lse, wo_own, wo_far, value_head):
    dma = pltpu.SemaphoreType.DMA
    anywhere = pl.BlockSpec(memory_space=pl.ANY)
    vmem = pl.BlockSpec(memory_space=pltpu.VMEM)
    return pl.pallas_call(
        finish_kernel,
        out_shape=(jax.ShapeDtypeStruct((256, 512), BF), jax.ShapeDtypeStruct((8, 256), F32)),
        in_specs=[vmem, vmem, anywhere, anywhere, vmem],
        out_specs=(vmem, vmem),
        scratch_shapes=[
            pltpu.VMEM((2048, 128), BF),
            pltpu.VMEM((8, 2, 128), F32),
            pltpu.VMEM((8, 512, 512), BF),
            pltpu.VMEM((8, 512, 512), BF),
            pltpu.VMEM((2048, 128), F32),
            pltpu.VMEM((2, 256, 512), BF),
            pltpu.VMEM((4, 4, 128, 512), BF),
            pltpu.VMEM((4, 4, 128, 512), BF),
            pltpu.VMEM((8, 256), F32),
            pltpu.VMEM((4, 8, 256), F32),
            pltpu.VMEM((8, 8, 256), F32),
            dma((4,)), dma((4,)), dma((1,)), dma((1,)), dma((2,)),
            dma((4, 4)), dma((4, 4)), dma((3,)), dma((3,)), dma((7,)), dma((7,)),
        ],
        compiler_params=pltpu.CompilerParams(
            collective_id=1, has_side_effects=True, vmem_limit_bytes=58 * MIB
        ),
        name="finish",
    )(o, lse, wo_own, wo_far, value_head)


def local(layer_in, q_weight, kv_weight, o_weight, kv_cache, cache_lengths, value_head):
    xh = lax.axis_index("tp") % 2
    x = layer_in[0].reshape(256, 512)
    qkv, wo_own, wo_far = project(x, q_weight[0], kv_weight[0], o_weight[0])
    spans = jnp.repeat(cache_lengths - xh * 256, 32).reshape(8, 2, 128)
    o, lse = attend(qkv, kv_cache[0], spans)
    hidden, gap = finish(o, lse, wo_own, wo_far, value_head.reshape(1, 512))
    hidden_out = hidden.reshape(1, 64, 4, 512)
    own_gap = lax.dynamic_slice_in_dim(gap[0].reshape(64, 4), 2 * lax.axis_index("sec"), 2, 1)
    return hidden_out, own_gap


def solution(mesh):
    placed = (
        P("sec", "grp", None, "tp"),
        P("sec", "grp", "tp"),
        P("sec", "grp", "tp"),
        P("sec", "tp", "grp"),
        P("sec", "grp", "tp", None),
        P("grp"),
        P("tp"),
    )
    return jax.shard_map(
        local,
        mesh=mesh,
        in_specs=placed,
        out_specs=(P("sec", "grp", None, "tp"), P("grp", "sec")),
        check_vma=False,
    )
```

```python
import functools

import jax
import jax.numpy as jnp
from jax import lax
from jax.experimental import pallas as pl
from jax.experimental.pallas import tpu as pltpu
from jax.sharding import PartitionSpec as P

HD = 128
CACHE = 512
MESH = pl.DeviceIdType.MESH
BF = jnp.bfloat16
F32 = jnp.float32
MIB = 1024 * 1024


def dot(a, b):
    return jnp.dot(a, b, preferred_element_type=F32)


def dot_nt(a, b):
    return lax.dot_general(a, b, (((1,), (1,)), ((), ())), preferred_element_type=F32)


def remote(src, dst, send, recv, **where):
    return pltpu.make_async_remote_copy(
        src_ref=src, dst_ref=dst, send_sem=send, recv_sem=recv, device_id=where, device_id_type=MESH
    )


def places():
    grp, tp = lax.axis_index("grp"), lax.axis_index("tp")
    return grp, tp, grp // 2, grp % 2, tp // 2, tp % 2


class OutputWeights:
    def __init__(self, src, full, y_send, y_recv, c_send, c_recv, own_sem):
        grp, tp, y, c, z, xh = places()
        self.grp, self.c, self.y = grp, c, y
        self.right, self.left = 2 * ((y + 1) % 4) + c, 2 * ((y + 3) % 4) + c
        self.src, self.full = src, full
        self.y_send, self.y_recv, self.c_send, self.c_recv, self.own_sem = y_send, y_recv, c_send, c_recv, own_sem

    def to_core(self, slot, src, place):
        return remote(src, self.full.at[place], self.c_send.at[slot], self.c_recv.at[slot], grp=self.grp ^ 1)

    def from_core(self, slot, place):
        return remote(
            self.full.at[place], self.full.at[place ^ 1], self.c_send.at[slot], self.c_recv.at[slot], grp=self.grp ^ 1
        )

    def one(self, which, place, src=None):
        to = self.right if which == 0 else self.left
        return remote(
            self.full.at[place] if src is None else src, self.full.at[place],
            self.y_send.at[which], self.y_recv.at[which], grp=to,
        )

    def half(self, which, place):
        to = self.right if which == 0 else self.left
        rows = pl.ds(256 * which, 256)
        return remote(
            self.full.at[place, rows], self.full.at[place, rows],
            self.y_send.at[2 + which], self.y_recv.at[2 + which], grp=to,
        )

    def start(self):
        self.own = pltpu.make_async_copy(self.src, self.full.at[self.grp], self.own_sem)
        self.own.start()
        self.sent = [self.one(0, self.grp, self.src), self.one(1, self.grp, self.src), self.to_core(0, self.src, self.grp)]
        for copy in self.sent:
            copy.start()

    def middle(self):
        for which, place in ((0, self.left), (1, self.right)):
            self.one(which, place).wait_recv()
            ahead = self.half(which, place)
            ahead.start()
            over = self.to_core(1 + which, self.full.at[place], place)
            over.start()
            self.sent += [ahead, over]

    def last(self):
        far = 2 * ((self.y + 2) % 4) + self.c
        for which in (0, 1):
            self.half(which, far).wait_recv()
        over = self.to_core(3, self.full.at[far], far)
        over.start()
        self.sent.append(over)

    def finish(self):
        self.own.wait()
        for copy in self.sent:
            copy.wait_send()
        for slot in range(4):
            self.from_core(slot, self.grp).wait_recv()


def project_kernel(
    x_hbm, wq_hbm, wkv_hbm, wo_hbm, qkv_out, wo_own, wo_far,
    xs, ws, mine, keep, to_core, from_core, to_y, from_y, final,
    perm_send, perm_recv, r_send, r_recv, l_send, l_recv, w_local, w_send, w_recv,
    c_send, c_recv, y_send, y_recv, a_send, a_recv, b_send, b_recv, own_sem,
    g_send, g_recv, h_send, h_recv, g_own, f_send, f_recv,
):
    grp, tp, y, c, z, xh = places()
    ring_r, ring_l = 2 * ((z + 1) % 8) + xh, 2 * ((z + 7) % 8) + xh
    dst_grp, dst_tp = z, 2 * (2 * y + xh) + c
    src_grp, src_tp = 2 * (z // 2) + xh, 2 * grp + z % 2
    stays = (dst_grp == grp) & (dst_tp == tp)
    moves = jnp.logical_not(stays)

    barrier = pltpu.get_barrier_semaphore()

    def greet(**where):
        pl.semaphore_signal(barrier, inc=1, device_id=where, device_id_type=MESH)

    @pl.when(moves)
    def _():
        greet(grp=dst_grp, tp=dst_tp)
        greet(grp=src_grp, tp=src_tp)

    greet(tp=ring_r)
    greet(tp=ring_l)
    greet(tp=tp ^ 1)
    greet(grp=grp ^ 1)
    greet(grp=grp ^ 1, tp=tp ^ 1)
    for d in (1, 2, 3):
        greet(grp=2 * ((y + d) % 4) + c)
    pl.semaphore_wait(barrier, jnp.where(moves, 10, 8))

    def rows(ch):
        return pl.ds(128 * ch, 128)

    def perm(ch):
        return remote(
            x_hbm.at[rows(ch)], xs.at[2 * y + xh, rows(ch)], perm_send.at[ch], perm_recv.at[ch], grp=dst_grp, tp=dst_tp
        )

    def perm_local(ch):
        return pltpu.make_async_copy(x_hbm.at[rows(ch)], xs.at[z, rows(ch)], perm_recv.at[ch])

    for ch in (0, 1):
        pl.when(moves)(lambda ch=ch: perm(ch).start())
        pl.when(stays)(lambda ch=ch: perm_local(ch).start())

    w_out = [
        remote(wq_hbm, ws.at[1, :, pl.ds(0, 512)], w_send.at[0], w_recv.at[0], tp=tp ^ 1),
        remote(wkv_hbm, ws.at[1, :, pl.ds(512, 128)], w_send.at[1], w_recv.at[1], tp=tp ^ 1),
    ]
    w_in = [
        pltpu.make_async_copy(wq_hbm, ws.at[0, :, pl.ds(0, 512)], w_local.at[0]),
        pltpu.make_async_copy(wkv_hbm, ws.at[0, :, pl.ds(512, 128)], w_local.at[1]),
    ]
    for copy in w_out + w_in:
        copy.start()
    wo = OutputWeights(
        wo_hbm.at[:, pl.ds(pl.multiple_of(512 * xh, 512), 512)], wo_own, g_send, g_recv, h_send, h_recv, g_own.at[0]
    )
    wo.start()

    def ring(right, k, ch, place):
        ss, rs, to = (r_send, r_recv, ring_r) if right else (l_send, l_recv, ring_l)
        block = xs.at[place, rows(ch)]
        return remote(block, block, ss.at[k - 1, ch], rs.at[k - 1, ch], tp=to)

    sent = []

    def send(copy):
        copy.start()
        sent.append(copy)

    def travels(right, k, ch):
        return k < 4 or (k == 4 and ch == (0 if right else 1))

    for ch in (0, 1):
        pl.when(moves)(lambda ch=ch: remote(
            x_hbm.at[rows(ch)], xs.at[z, rows(ch)], perm_send.at[ch], perm_recv.at[ch], grp=dst_grp, tp=dst_tp
        ).wait_recv())
        pl.when(stays)(lambda ch=ch: perm_local(ch).wait())
        for right in (True, False):
            send(ring(right, 1, ch, z))

    even = z % 2 == 0
    pair = z // 2
    order = [
        pair,
        jnp.where(even, pair + 3, pair + 1) % 4,
        jnp.where(even, pair + 1, pair + 3) % 4,
        (pair + 2) % 4,
    ]

    def product(j, yp, half):
        block = pl.ds(pl.multiple_of(128 * half, 128), 128)
        return dot(xs[2 * yp, block, :], ws[j, :512, :]) + dot(xs[2 * yp + 1, block, :], ws[j, 512:, :])

    def core_copy(j, i):
        return remote(to_core.at[j, i], from_core.at[j, i], c_send.at[j, i], c_recv.at[j, i], grp=grp ^ 1)

    def compute(j, i):
        to_core[j, i] = product(j, order[i], c ^ 1).astype(BF)
        send(core_copy(j, i))
        mine[j, i] = product(j, order[i], c)

    def y_copy(j, i, d):
        return remote(
            to_y.at[j, i], from_y.at[j, d - 1], y_send.at[j, i], y_recv.at[j, d - 1],
            grp=2 * ((y + d) % 4) + c,
        )

    def pass_on(j, i):
        core_copy(j, i).wait_recv()
        total = mine[j, i] + from_core[j, i].astype(F32)
        d = (order[i] - y + 4) % 4

        @pl.when(d == 0)
        def _():
            keep[j] = total

        @pl.when(d != 0)
        def _():
            to_y[j, i] = total.astype(BF)
            y_copy(j, i, d).start()

    for copy in w_in:
        copy.wait()
    for k in (1, 2, 3, 4):
        for ch in (0, 1):
            for right in (True, False):
                if not travels(right, k, ch):
                    continue
                place = (z + 8 - k) % 8 if right else (z + k) % 8
                ring(right, k, ch, place).wait_recv()
                if k < 4 and travels(right, k + 1, ch):
                    send(ring(right, k + 1, ch, place))
        compute(0, k - 1)
        if k > 1:
            pass_on(0, k - 2)
        if k == 2:
            wo.middle()
    pass_on(0, 3)
    for copy in w_out:
        copy.wait_recv()
    far_cols = pl.ds(pl.multiple_of(512 * (xh ^ 1), 512), 512)
    far = remote(wo_hbm.at[:, far_cols], wo_far, f_send.at[0], f_recv.at[0], tp=tp ^ 1)
    far.start()
    for i in range(4):
        compute(1, i)
        if i > 0:
            pass_on(1, i - 1)
    pass_on(1, 3)
    wo.last()

    near = c == xh

    def place_of(cols, half):
        return qkv_out.at[cols, pl.ds(pl.multiple_of(128 * half, 128), 128)]

    for j in (0, 1):
        total = keep[j]
        for d in (1, 2, 3):
            remote(to_y.at[j, 0], from_y.at[j, d - 1], y_send.at[j, 0], y_recv.at[j, d - 1], grp=grp).wait_recv()
            total = total + from_y[j, d - 1].astype(F32)
        final[j] = total.astype(BF)
        spot = place_of(xh ^ j, c)

        @pl.when(near)
        def _():
            pltpu.make_async_copy(final.at[j], spot, own_sem.at[j]).start()

        @pl.when(jnp.logical_not(near))
        def _():
            remote(final.at[j], spot, a_send.at[j], a_recv.at[j], grp=grp ^ 1).start()

        remote(final.at[j], spot, b_send.at[j], b_recv.at[j, c], grp=2 * y + xh, tp=tp ^ 1).start()

    for j in (0, 1):
        spot = place_of(xh ^ j, c)

        @pl.when(near)
        def _():
            pltpu.make_async_copy(final.at[j], spot, own_sem.at[j]).wait()
            remote(final.at[j], place_of(xh ^ j, c ^ 1), a_send.at[j], a_recv.at[j], grp=grp ^ 1).wait_recv()

        @pl.when(jnp.logical_not(near))
        def _():
            remote(final.at[j], spot, a_send.at[j], a_recv.at[j], grp=grp ^ 1).wait_send()
            for half in (0, 1):
                remote(
                    final.at[j], place_of(xh ^ 1 ^ j, half), b_send.at[j], b_recv.at[j, half],
                    grp=2 * y + xh, tp=tp ^ 1,
                ).wait_recv()

        remote(final.at[j], spot, b_send.at[j], b_recv.at[j, c], grp=2 * y + xh, tp=tp ^ 1).wait_send()

    for copy in sent:
        copy.wait_send()
    for copy in w_out:
        copy.wait_send()
    for ch in (0, 1):
        pl.when(moves)(lambda ch=ch: perm(ch).wait_send())
    for j in (0, 1):
        for i in range(4):
            d = (order[i] - y + 4) % 4
            pl.when(d != 0)(lambda j=j, i=i, d=d: y_copy(j, i, d).wait_send())
    wo.finish()
    far.wait()


def project(x, wq, wkv, wo):
    dma = pltpu.SemaphoreType.DMA
    anywhere = pl.BlockSpec(memory_space=pl.ANY)
    return pl.pallas_call(
        project_kernel,
        out_shape=(
            jax.ShapeDtypeStruct((2, 256, 640), BF),
            jax.ShapeDtypeStruct((8, 512, 512), BF),
            jax.ShapeDtypeStruct((512, 512), BF),
        ),
        in_specs=[anywhere] * 4,
        out_specs=(anywhere,) * 3,
        scratch_shapes=[
            pltpu.VMEM((8, 256, 512), BF),
            pltpu.VMEM((2, 1024, 640), BF),
            pltpu.VMEM((2, 4, 128, 640), F32),
            pltpu.VMEM((2, 128, 640), F32),
            pltpu.VMEM((2, 4, 128, 640), BF),
            pltpu.VMEM((2, 4, 128, 640), BF),
            pltpu.VMEM((2, 4, 128, 640), BF),
            pltpu.VMEM((2, 3, 128, 640), BF),
            pltpu.VMEM((2, 128, 640), BF),
            dma((2,)), dma((2,)), dma((4, 2)), dma((4, 2)), dma((4, 2)), dma((4, 2)), dma((2,)), dma((2,)), dma((2,)),
            dma((2, 4)), dma((2, 4)), dma((2, 4)), dma((2, 3)), dma((2,)), dma((2,)), dma((2,)), dma((2, 2)), dma((2,)),
            dma((4,)), dma((4,)), dma((4,)), dma((4,)), dma((1,)), dma((1,)), dma((1,)),
        ],
        compiler_params=pltpu.CompilerParams(
            collective_id=0, has_side_effects=True, vmem_limit_bytes=58 * MIB
        ),
        name="project",
    )(x, wq, wkv, wo)


def attend(group, q_ref, kv_ref, len_ref, out_ref, lse_ref, q_rows, leader):
    scale = HD ** -0.5
    lane = lax.broadcasted_iota(jnp.int32, (1, 128), 1)
    pos = lax.broadcasted_iota(jnp.int32, (256, 128), 0)
    lane_roll, lane_step = lane // 32, lane % 32 // 8
    new_row = lax.broadcasted_iota(jnp.int32, (16, 128), 0)
    causal = (new_row // 4 == lane_roll) & (new_row % 4 <= lane_step) & leader
    tokens = pl.ds(pl.multiple_of(16 * group, 16), 16)
    for part in (0, 1):
        vals = q_ref[part, tokens, :].astype(F32)
        for head in range(4):
            q_rows[pl.ds(4 * part + head, 16, stride=8), :] = vals[:, 128 * head:128 * head + 128]
    new_key = q_ref[0, tokens, 512:]
    new_val = q_ref[1, tokens, 512:]
    q_t = q_rows[...].T.astype(BF)
    cached = None
    for i in range(4):
        one = dot(kv_ref[4 * group + i, :, :128], q_t)
        cached = one if cached is None else jnp.where(lane_roll == i, one, cached)
    visible = pos < len_ref[group]
    cached = jnp.where(visible, cached * scale, -1e30)
    fresh = jnp.where(causal, dot(new_key, q_t) * scale, -1e30)
    peak = jnp.maximum(jnp.max(cached, axis=0, keepdims=True), jnp.max(fresh, axis=0, keepdims=True))
    cached = jnp.where(visible, jnp.exp(cached - peak), 0.0)
    fresh = jnp.where(causal, jnp.exp(fresh - peak), 0.0)
    total = jnp.sum(cached, axis=0, keepdims=True) + jnp.sum(fresh, axis=0, keepdims=True)
    lse_ref[group] = jnp.where(total > 0.0, peak + jnp.log(jnp.maximum(total, 1e-30)), -1e30)
    inverse = jnp.where(total > 0.0, 1.0 / jnp.maximum(total, 1e-30), 0.0)
    weights = (cached * inverse).T.astype(BF)
    fresh_w = jnp.concatenate([fresh * inverse, jnp.zeros((112, 128), F32)], axis=0).T.astype(BF)
    new_pad = jnp.concatenate([new_val, jnp.zeros((112, 128), BF)], axis=0)
    added = dot(fresh_w, new_pad)
    for i in range(4):
        block = slice(32 * i, 32 * i + 32)
        got = dot(weights[block], kv_ref[4 * group + i, :, 128:]) + added[block]
        out_ref[pl.ds(pl.multiple_of(128 * group + 32 * i, 32), 32), :] = got.astype(BF)


def finish_kernel(
    q_ref, kv_hbm, len_ref, wo_own_hbm, wo_far_hbm, head_ref, hidden_out, gap_out,
    kv, q_rows, o_own, lse_own, o_got, lse_got, near_w, far_w, merged, ctx, outgo, income, gap_own, gaps_all,
    kv_sem, o_send, o_recv, s_send, s_recv, near_sem, ring_send, ring_recv, gap_send, gap_recv,
    g_send, g_recv, h_send, h_recv, g_own,
):
    grp, tp, y, c, z, xh = places()
    sec = lax.axis_index("sec")
    barrier = pltpu.get_barrier_semaphore()

    def others():
        for d in range(1, 32):
            yield d - 1, dict(tp=(tp + d % 16) % 16, sec=sec ^ (d // 16))

    for _, where in others():
        pl.semaphore_signal(barrier, inc=1, device_id=where, device_id_type=MESH)
    for away in (grp ^ 1, 2 * ((y + 1) % 4) + c, 2 * ((y + 3) % 4) + c):
        pl.semaphore_signal(barrier, inc=1, device_id={"grp": away}, device_id_type=MESH)

    def cache_copy(n):
        rollouts = pl.ds(pl.multiple_of(8 * n, 8), 8)
        return pltpu.make_async_copy(kv_hbm.at[rollouts], kv.at[rollouts], kv_sem.at[n])

    for n in range(8):
        cache_copy(n).start()
    near = pltpu.make_async_copy(wo_own_hbm, near_w, near_sem.at[0])
    near.start()
    wo = OutputWeights(wo_far_hbm, far_w, g_send, g_recv, h_send, h_recv, g_own.at[0])
    pl.semaphore_wait(barrier, 34)
    wo.start()

    def attend_part(n):
        def body(m, carry):
            cache_copy(m).wait()
            for lane in (0, 1):
                attend(2 * m + lane, q_ref, kv, len_ref, o_own, lse_own, q_rows.at[lane], xh == 0)
            return carry

        lax.fori_loop(2 * n, 2 * n + 2, body, 0)

    def o_copy(n):
        block = pl.ds(512 * n, 512)
        return remote(o_own.at[block], o_got.at[block], o_send.at[n], o_recv.at[n], tp=tp ^ 1)

    def lse_copy(n):
        block = pl.ds(4 * n, 4)
        return remote(lse_own.at[block], lse_got.at[block], s_send.at[n], s_recv.at[n], tp=tp ^ 1)

    def merge(n):
        lse_copy(n).wait_recv()
        o_copy(n).wait_recv()
        for m in range(4 * n, 4 * n + 4):
            factor = 1.0 / (1.0 + jnp.exp(lse_got[m] - lse_own[m]))
            factor = jnp.broadcast_to(factor, (128, 128)).T
            block = slice(128 * m, 128 * m + 128)
            own = o_own[block, :].astype(F32)
            got = o_got[block, :].astype(F32)
            merged[block, :] = own * factor + got * (1.0 - factor)
        for part in (0, 1):
            for head in range(4):
                ctx[part, pl.ds(64 * n, 64), pl.ds(128 * head, 128)] = merged[
                    pl.ds(512 * n + 4 * part + head, 64, stride=8), :
                ].astype(BF)

    for n in range(4):
        attend_part(n)
        lse_copy(n).start()
        o_copy(n).start()
        if n > 1:
            merge(n - 2)
        if n == 3:
            wo.middle()
    merge(2)
    merge(3)
    near.wait()
    wo.last()
    wo.finish()

    def block(place, ch):
        return dot(ctx[xh, 128 * ch:128 * ch + 128, :], near_w[place]) + dot(
            ctx[xh ^ 1, 128 * ch:128 * ch + 128, :], far_w[place]
        )

    def slot(right, ch):
        return 2 * ch + (0 if right else 1)

    def ring(right, ch, k):
        s = slot(right, ch)
        to = 2 * ((z + (1 if right else 7)) % 8) + xh
        return remote(outgo.at[s, k - 1], income.at[s, k - 1], ring_send.at[s, k - 1], ring_recv.at[s, k - 1], tp=to)

    sent = []

    def longest(right, ch):
        return 4 if ch == (0 if right else 1) else 3

    for turn in range(4):
        for right, ch in ((True, 0), (False, 1), (True, 1), (False, 0)):
            k = longest(right, ch) - turn
            if k < 1:
                continue
            place = (z + k) % 8 if right else (z + 8 - k) % 8
            total = block(place, ch)
            if turn > 0:
                ring(right, ch, k + 1).wait_recv()
                total = total + income[slot(right, ch), k].astype(F32)
            outgo[slot(right, ch), k - 1] = total.astype(BF)
            copy = ring(right, ch, k)
            copy.start()
            sent.append(copy)

    value = head_ref[...]
    first = value.astype(BF)
    rest = value - first.astype(F32)
    second = rest.astype(BF)
    third = (rest - second.astype(F32)).astype(BF)
    which = lax.broadcasted_iota(jnp.int32, (16, 512), 0)
    triple = jnp.where(
        which == 0, first.astype(F32),
        jnp.where(which == 1, second.astype(F32), jnp.where(which == 2, third.astype(F32), 0.0)),
    ).astype(BF)
    gaps = []
    for ch in (0, 1):
        total = block(z, ch)
        for right in (True, False):
            ring(right, ch, 1).wait_recv()
            total = total + income[slot(right, ch), 0].astype(F32)
        result = total.astype(BF)
        hidden_out[128 * ch:128 * ch + 128, :] = result
        gaps.append(jnp.sum(dot_nt(triple, result), axis=0, keepdims=True))
    gap = jnp.concatenate(gaps + [jnp.zeros((6, 128), F32)], axis=0)
    gap = jnp.where(sec == 0, gap, -gap)
    own_place = 16 * sec + tp
    gap_own[...] = gap
    gaps_all[own_place] = gap

    def gap_copy(n, where):
        return remote(gap_own, gaps_all.at[own_place], gap_send.at[n], gap_recv.at[n], **where)

    for n, where in others():
        gap_copy(n, where).start()
    for n, where in others():
        gap_copy(n, where).wait_recv()
    total = gaps_all[0]
    for n in range(1, 32):
        total = total + gaps_all[n]
    gap_out[...] = total

    for n, where in others():
        gap_copy(n, where).wait_send()
    for copy in sent:
        copy.wait_send()
    for n in range(4):
        lse_copy(n).wait_send()
        o_copy(n).wait_send()


def finish(qkv, cache, spans, wo_own, wo_far, value_head):
    dma = pltpu.SemaphoreType.DMA
    anywhere = pl.BlockSpec(memory_space=pl.ANY)
    vmem = pl.BlockSpec(memory_space=pltpu.VMEM)
    return pl.pallas_call(
        finish_kernel,
        out_shape=(jax.ShapeDtypeStruct((256, 512), BF), jax.ShapeDtypeStruct((8, 128), F32)),
        in_specs=[vmem, anywhere, vmem, anywhere, anywhere, vmem],
        out_specs=(vmem, vmem),
        scratch_shapes=[
            pltpu.VMEM((64, 256, 256), BF),
            pltpu.VMEM((2, 128, 128), F32),
            pltpu.VMEM((2048, 128), BF),
            pltpu.VMEM((16, 1, 128), F32),
            pltpu.VMEM((2048, 128), BF),
            pltpu.VMEM((16, 1, 128), F32),
            pltpu.VMEM((8, 512, 512), BF),
            pltpu.VMEM((8, 512, 512), BF),
            pltpu.VMEM((2048, 128), F32),
            pltpu.VMEM((2, 256, 512), BF),
            pltpu.VMEM((4, 4, 128, 512), BF),
            pltpu.VMEM((4, 4, 128, 512), BF),
            pltpu.VMEM((8, 128), F32),
            pltpu.VMEM((32, 8, 128), F32),
            dma((8,)), dma((4,)), dma((4,)), dma((4,)), dma((4,)), dma((1,)),
            dma((4, 4)), dma((4, 4)), dma((31,)), dma((31,)),
            dma((4,)), dma((4,)), dma((4,)), dma((4,)), dma((1,)),
        ],
        compiler_params=pltpu.CompilerParams(
            collective_id=1, has_side_effects=True, vmem_limit_bytes=58 * MIB
        ),
        name="finish",
    )(qkv, cache, spans, wo_own, wo_far, value_head)


def local(layer_in, q_weight, kv_weight, o_weight, kv_cache, cache_lengths, value_head):
    xh = lax.axis_index("tp") % 2
    x = layer_in[0].reshape(256, 512)
    qkv, wo_own, wo_far = project(x, q_weight[0], kv_weight[0], o_weight[0])
    spans = jnp.repeat(cache_lengths - xh * 256, 32).reshape(16, 1, 128)
    hidden, gap = finish(qkv, kv_cache[0], spans, wo_own, wo_far, value_head.reshape(1, 512))
    hidden_out = hidden.reshape(1, 64, 4, 512)
    own_gap = lax.dynamic_slice_in_dim(gap[:2].reshape(64, 4), 2 * lax.axis_index("sec"), 2, 1)
    return hidden_out, own_gap


def solution(mesh):
    placed = (
        P("sec", "grp", None, "tp"),
        P("sec", "grp", "tp"),
        P("sec", "grp", "tp"),
        P("sec", "tp", "grp"),
        P("sec", "grp", "tp", None),
        P("grp"),
        P("tp"),
    )
    return jax.shard_map(
        local,
        mesh=mesh,
        in_specs=placed,
        out_specs=(P("sec", "grp", None, "tp"), P("grp", "sec")),
        check_vma=False,
    )
```

```python
import functools

import jax
import jax.numpy as jnp
from jax import lax
from jax.experimental import pallas as pl
from jax.experimental.pallas import tpu as pltpu
from jax.sharding import PartitionSpec as P

HD = 128
CACHE = 512
MESH = pl.DeviceIdType.MESH
BF = jnp.bfloat16
F32 = jnp.float32
MIB = 1024 * 1024


def dot(a, b):
    return jnp.dot(a, b, preferred_element_type=F32)


def dot_nt(a, b):
    return lax.dot_general(a, b, (((1,), (1,)), ((), ())), preferred_element_type=F32)


def remote(src, dst, send, recv, **where):
    return pltpu.make_async_remote_copy(
        src_ref=src, dst_ref=dst, send_sem=send, recv_sem=recv, device_id=where, device_id_type=MESH
    )


def places():
    grp, tp = lax.axis_index("grp"), lax.axis_index("tp")
    return grp, tp, grp // 2, grp % 2, tp // 2, tp % 2


class OutputWeights:
    def __init__(self, src, full, y_send, y_recv, c_send, c_recv, own_sem):
        grp, tp, y, c, z, xh = places()
        self.grp, self.c, self.y = grp, c, y
        self.right, self.left = 2 * ((y + 1) % 4) + c, 2 * ((y + 3) % 4) + c
        self.src, self.full = src, full
        self.y_send, self.y_recv, self.c_send, self.c_recv, self.own_sem = y_send, y_recv, c_send, c_recv, own_sem

    def to_core(self, slot, src, place):
        return remote(src, self.full.at[place], self.c_send.at[slot], self.c_recv.at[slot], grp=self.grp ^ 1)

    def from_core(self, slot, place):
        return remote(
            self.full.at[place], self.full.at[place ^ 1], self.c_send.at[slot], self.c_recv.at[slot], grp=self.grp ^ 1
        )

    def one(self, which, place, src=None):
        to = self.right if which == 0 else self.left
        return remote(
            self.full.at[place] if src is None else src, self.full.at[place],
            self.y_send.at[which], self.y_recv.at[which], grp=to,
        )

    def half(self, which, place):
        to = self.right if which == 0 else self.left
        rows = pl.ds(256 * which, 256)
        return remote(
            self.full.at[place, rows], self.full.at[place, rows],
            self.y_send.at[2 + which], self.y_recv.at[2 + which], grp=to,
        )

    def start(self):
        self.own = pltpu.make_async_copy(self.src, self.full.at[self.grp], self.own_sem)
        self.own.start()
        self.sent = [self.one(0, self.grp, self.src), self.one(1, self.grp, self.src), self.to_core(0, self.src, self.grp)]
        for copy in self.sent:
            copy.start()

    def middle(self):
        for which, place in ((0, self.left), (1, self.right)):
            self.one(which, place).wait_recv()
            ahead = self.half(which, place)
            ahead.start()
            over = self.to_core(1 + which, self.full.at[place], place)
            over.start()
            self.sent += [ahead, over]

    def last(self):
        far = 2 * ((self.y + 2) % 4) + self.c
        for which in (0, 1):
            self.half(which, far).wait_recv()
        over = self.to_core(3, self.full.at[far], far)
        over.start()
        self.sent.append(over)

    def finish(self):
        self.own.wait()
        for copy in self.sent:
            copy.wait_send()
        for slot in range(4):
            self.from_core(slot, self.grp).wait_recv()


def project(
    x_hbm, wq_hbm, wkv_hbm, wo_hbm, qkv_out, wo_own, swapped, wo_far, begin,
    xs, ws, mine, keep, to_core, from_core, to_y, from_y, final,
    perm_send, perm_recv, r_send, r_recv, l_send, l_recv, w_local, w_send, w_recv,
    c_send, c_recv, y_send, y_recv, a_send, a_recv, b_send, b_recv, own_sem,
    g_send, g_recv, h_send, h_recv, g_own, f_send, f_recv, i_send, i_recv, j_send, j_recv, i_own,
):
    grp, tp, y, c, z, xh = places()
    ring_r, ring_l = 2 * ((z + 1) % 8) + xh, 2 * ((z + 7) % 8) + xh
    spot = (z - 2 * y - 4 * xh + 16) % 8
    dst_grp, dst_tp = z, 2 * ((2 * (z // 2) + 2 * y + xh + 4 * c) % 8) + c
    src_grp, src_tp = 2 * (spot // 2) + xh, 2 * grp + spot % 2
    stays = (dst_grp == grp) & (dst_tp == tp)
    moves = jnp.logical_not(stays)

    barrier = pltpu.get_barrier_semaphore()

    def greet(**where):
        pl.semaphore_signal(barrier, inc=1, device_id=where, device_id_type=MESH)

    @pl.when(moves)
    def _():
        greet(grp=dst_grp, tp=dst_tp)
        greet(grp=src_grp, tp=src_tp)

    sec = lax.axis_index("sec")
    greet(tp=tp ^ 1)
    greet(sec=sec ^ 1)
    greet(tp=tp ^ 1, sec=sec ^ 1)
    for d in range(1, 8):
        greet(tp=2 * ((z + d) % 8) + xh)
    greet(grp=grp ^ 1)
    greet(grp=grp ^ 1, tp=tp ^ 1)
    for d in (1, 2, 3):
        greet(grp=2 * ((y + d) % 4) + c)
    pl.semaphore_wait(barrier, jnp.where(moves, 17, 15))

    def rows(ch):
        return pl.ds(128 * ch, 128)

    def perm(ch):
        return remote(
            x_hbm.at[rows(ch)], xs.at[2 * y + xh, rows(ch)], perm_send.at[ch], perm_recv.at[ch], grp=dst_grp, tp=dst_tp
        )

    def perm_local(ch):
        return pltpu.make_async_copy(x_hbm.at[rows(ch)], xs.at[spot, rows(ch)], perm_recv.at[ch])

    for ch in (0, 1):
        pl.when(moves)(lambda ch=ch: perm(ch).start())
        pl.when(stays)(lambda ch=ch: perm_local(ch).start())

    w_out = [
        remote(wq_hbm, ws.at[1, :, pl.ds(0, 512)], w_send.at[0], w_recv.at[0], tp=tp ^ 1),
        remote(wkv_hbm, ws.at[1, :, pl.ds(512, 128)], w_send.at[1], w_recv.at[1], tp=tp ^ 1),
    ]
    w_in = [
        pltpu.make_async_copy(wq_hbm, ws.at[0, :, pl.ds(0, 512)], w_local.at[0]),
        pltpu.make_async_copy(wkv_hbm, ws.at[0, :, pl.ds(512, 128)], w_local.at[1]),
    ]
    for copy in w_out + w_in:
        copy.start()
    wo = OutputWeights(
        wo_hbm.at[:, pl.ds(pl.multiple_of(512 * xh, 512), 512)], wo_own, g_send, g_recv, h_send, h_recv, g_own.at[0]
    )
    wo.start()
    wo2 = OutputWeights(swapped, wo_far, i_send, i_recv, j_send, j_recv, i_own.at[0])
    begin()

    def ring(right, k, ch, place):
        ss, rs, to = (r_send, r_recv, ring_r) if right else (l_send, l_recv, ring_l)
        block = xs.at[place, rows(ch)]
        return remote(block, block, ss.at[k - 1, ch], rs.at[k - 1, ch], tp=to)

    sent = []

    def send(copy):
        copy.start()
        sent.append(copy)

    def travels(right, k, ch):
        return k < 4 or (k == 4 and ch == (0 if right else 1))

    for ch in (0, 1):
        pl.when(moves)(lambda ch=ch: remote(
            x_hbm.at[rows(ch)], xs.at[spot, rows(ch)], perm_send.at[ch], perm_recv.at[ch], grp=dst_grp, tp=dst_tp
        ).wait_recv())
        pl.when(stays)(lambda ch=ch: perm_local(ch).wait())
        for right in (True, False):
            send(ring(right, 1, ch, spot))

    even = spot % 2 == 0
    pair = spot // 2
    order = [
        pair,
        jnp.where(even, pair + 3, pair + 1) % 4,
        jnp.where(even, pair + 1, pair + 3) % 4,
        (pair + 2) % 4,
    ]

    def product(j, yp, half):
        block = pl.ds(pl.multiple_of(128 * half, 128), 128)
        return dot(xs[2 * yp, block, :], ws[j, :512, :]) + dot(xs[2 * yp + 1, block, :], ws[j, 512:, :])

    def core_copy(j, i):
        return remote(to_core.at[j, i], from_core.at[j, i], c_send.at[j, i], c_recv.at[j, i], grp=grp ^ 1)

    def compute(j, i):
        to_core[j, i] = product(j, order[i], c ^ 1).astype(BF)
        send(core_copy(j, i))
        mine[j, i] = product(j, order[i], c)

    def y_copy(j, i, d):
        return remote(
            to_y.at[j, i], from_y.at[j, d - 1], y_send.at[j, i], y_recv.at[j, d - 1],
            grp=2 * ((y + d) % 4) + c,
        )

    def pass_on(j, i):
        core_copy(j, i).wait_recv()
        total = mine[j, i] + from_core[j, i].astype(F32)
        d = (order[i] - y + 4) % 4

        @pl.when(d == 0)
        def _():
            keep[j] = total

        @pl.when(d != 0)
        def _():
            to_y[j, i] = total.astype(BF)
            y_copy(j, i, d).start()

    for copy in w_in:
        copy.wait()
    for k in (1, 2, 3, 4):
        for ch in (0, 1):
            for right in (True, False):
                if not travels(right, k, ch):
                    continue
                place = (spot + 8 - k) % 8 if right else (spot + k) % 8
                ring(right, k, ch, place).wait_recv()
                if k < 4 and travels(right, k + 1, ch):
                    send(ring(right, k + 1, ch, place))
        if k < 4:
            compute(0, k - 1)
        if k == 2:
            pass_on(0, 0)
            wo.middle()
        if k == 3:
            pass_on(0, 1)
            for copy in w_out:
                copy.wait_recv()
            far_cols = pl.ds(pl.multiple_of(512 * (xh ^ 1), 512), 512)
            far = remote(wo_hbm.at[:, far_cols], swapped, f_send.at[0], f_recv.at[0], tp=tp ^ 1)
            far.start()
            compute(1, 0)
            compute(1, 1)
            pass_on(0, 2)
            compute(1, 2)
            wo.last()
            pass_on(1, 0)
            pass_on(1, 1)
    compute(0, 3)
    compute(1, 3)
    pass_on(1, 2)
    pass_on(0, 3)
    pass_on(1, 3)

    near = c == xh

    def place_of(cols, half):
        return qkv_out.at[cols, pl.ds(pl.multiple_of(128 * half, 128), 128)]

    for j in (0, 1):
        total = keep[j]
        for d in (1, 2, 3):
            remote(to_y.at[j, 0], from_y.at[j, d - 1], y_send.at[j, 0], y_recv.at[j, d - 1], grp=grp).wait_recv()
            total = total + from_y[j, d - 1].astype(F32)
        final[j] = total.astype(BF)
        spot = place_of(xh ^ j, c)

        @pl.when(near)
        def _():
            pltpu.make_async_copy(final.at[j], spot, own_sem.at[j]).start()

        @pl.when(jnp.logical_not(near))
        def _():
            remote(final.at[j], spot, a_send.at[j], a_recv.at[j], grp=grp ^ 1).start()

        remote(final.at[j], spot, b_send.at[j], b_recv.at[j, c], grp=2 * y + xh, tp=tp ^ 1).start()

    far.wait_recv()
    wo2.start()
    for j in (0, 1):
        spot = place_of(xh ^ j, c)

        @pl.when(near)
        def _():
            pltpu.make_async_copy(final.at[j], spot, own_sem.at[j]).wait()
            remote(final.at[j], place_of(xh ^ j, c ^ 1), a_send.at[j], a_recv.at[j], grp=grp ^ 1).wait_recv()

        @pl.when(jnp.logical_not(near))
        def _():
            remote(final.at[j], spot, a_send.at[j], a_recv.at[j], grp=grp ^ 1).wait_send()
            for half in (0, 1):
                remote(
                    final.at[j], place_of(xh ^ 1 ^ j, half), b_send.at[j], b_recv.at[j, half],
                    grp=2 * y + xh, tp=tp ^ 1,
                ).wait_recv()

    def drain():
        for j in (0, 1):
            remote(
                final.at[j], place_of(xh ^ j, c), b_send.at[j], b_recv.at[j, c], grp=2 * y + xh, tp=tp ^ 1
            ).wait_send()
        for copy in sent:
            copy.wait_send()
        for copy in w_out:
            copy.wait_send()
        for ch in (0, 1):
            pl.when(moves)(lambda ch=ch: perm(ch).wait_send())
        for j in (0, 1):
            for i in range(4):
                d = (order[i] - y + 4) % 4
                pl.when(d != 0)(lambda j=j, i=i, d=d: y_copy(j, i, d).wait_send())
        far.wait_send()

    return wo, wo2, drain


def attend(group, q_ref, kv_ref, len_ref, out_ref, lse_ref, q_rows, xh):
    scale = HD ** -0.5
    lane = lax.broadcasted_iota(jnp.int32, (1, 128), 1)
    pos = lax.broadcasted_iota(jnp.int32, (256, 128), 0)
    lane_roll, lane_step = lane // 32, lane % 32 // 8
    new_row = lax.broadcasted_iota(jnp.int32, (16, 128), 0)
    causal = (new_row // 4 == lane_roll) & (new_row % 4 <= lane_step) & (xh == 0)
    tokens = pl.ds(pl.multiple_of(16 * group, 16), 16)
    for part in (0, 1):
        vals = q_ref[part, tokens, :].astype(F32)
        for head in range(4):
            q_rows[pl.ds(4 * part + head, 16, stride=8), :] = vals[:, 128 * head:128 * head + 128]
    new_key = q_ref[0, tokens, 512:]
    new_val = q_ref[1, tokens, 512:]
    q_t = q_rows[...].T.astype(BF)
    cached = None
    for i in range(4):
        one = dot(kv_ref[4 * group + i, :, :128], q_t)
        cached = one if cached is None else jnp.where(lane_roll == i, one, cached)
    span = jnp.zeros((1, 128), jnp.int32)
    for i in range(4):
        span = jnp.where(lane_roll == i, len_ref[4 * group + i], span)
    visible = pos < span - 256 * xh
    cached = jnp.where(visible, cached * scale, -1e30)
    fresh = jnp.where(causal, dot(new_key, q_t) * scale, -1e30)
    peak = jnp.maximum(jnp.max(cached, axis=0, keepdims=True), jnp.max(fresh, axis=0, keepdims=True))
    cached = jnp.where(visible, jnp.exp(cached - peak), 0.0)
    fresh = jnp.where(causal, jnp.exp(fresh - peak), 0.0)
    total = jnp.sum(cached, axis=0, keepdims=True) + jnp.sum(fresh, axis=0, keepdims=True)
    lse_ref[group] = jnp.where(total > 0.0, peak + jnp.log(jnp.maximum(total, 1e-30)), -1e30)
    inverse = jnp.where(total > 0.0, 1.0 / jnp.maximum(total, 1e-30), 0.0)
    weights = (cached * inverse).T.astype(BF)
    fresh_w = jnp.concatenate([fresh * inverse, jnp.zeros((112, 128), F32)], axis=0).T.astype(BF)
    new_pad = jnp.concatenate([new_val, jnp.zeros((112, 128), BF)], axis=0)
    added = dot(fresh_w, new_pad)
    for i in range(4):
        block = slice(32 * i, 32 * i + 32)
        got = dot(weights[block], kv_ref[4 * group + i, :, 128:]) + added[block]
        out_ref[pl.ds(pl.multiple_of(128 * group + 32 * i, 32), 32), :] = got.astype(BF)


def finish(
    q_ref, cache_copy, len_ref, wo, wo2, head_ref, hidden_out, gap_out,
    kv, q_rows, o_own, lse_own, o_got, lse_got, near_w, far_w, merged, ctx, outgo, income, gap_own, gap_x, gap_z,
    o_send, o_recv, s_send, s_recv, ring_send, ring_recv, gx_send, gx_recv, gz_send, gz_recv,
):
    grp, tp, y, c, z, xh = places()
    sec = lax.axis_index("sec")

    def attend_part(n):
        def body(m, carry):
            cache_copy(m).wait()
            for lane in (0, 1):
                attend(2 * m + lane, q_ref, kv, len_ref, o_own, lse_own, q_rows.at[lane], xh)
            return carry

        lax.fori_loop(2 * n, 2 * n + 2, body, 0)

    def o_copy(n):
        block = pl.ds(512 * n, 512)
        return remote(o_own.at[block], o_got.at[block], o_send.at[n], o_recv.at[n], tp=tp ^ 1)

    def lse_copy(n):
        block = pl.ds(4 * n, 4)
        return remote(lse_own.at[block], lse_got.at[block], s_send.at[n], s_recv.at[n], tp=tp ^ 1)

    def merge(n):
        lse_copy(n).wait_recv()
        o_copy(n).wait_recv()
        for m in range(4 * n, 4 * n + 4):
            factor = 1.0 / (1.0 + jnp.exp(lse_got[m] - lse_own[m]))
            factor = jnp.broadcast_to(factor, (128, 128)).T
            block = slice(128 * m, 128 * m + 128)
            own = o_own[block, :].astype(F32)
            got = o_got[block, :].astype(F32)
            merged[block, :] = own * factor + got * (1.0 - factor)
        for part in (0, 1):
            for head in range(4):
                ctx[part, pl.ds(64 * n, 64), pl.ds(128 * head, 128)] = merged[
                    pl.ds(512 * n + 4 * part + head, 64, stride=8), :
                ].astype(BF)

    for n in range(4):
        attend_part(n)
        lse_copy(n).start()
        o_copy(n).start()
        if n == 1:
            wo2.middle()
        if n > 1:
            merge(n - 2)
    wo2.last()
    wo.finish()
    wo2.finish()

    def block(place, ch):
        return dot(ctx[xh, 128 * ch:128 * ch + 128, :], near_w[place]) + dot(
            ctx[xh ^ 1, 128 * ch:128 * ch + 128, :], far_w[place]
        )

    def slot(right, ch):
        return 2 * ch + (0 if right else 1)

    def ring(right, ch, k):
        s = slot(right, ch)
        to = 2 * ((z + (1 if right else 7)) % 8) + xh
        return remote(outgo.at[s, k - 1], income.at[s, k - 1], ring_send.at[s, k - 1], ring_recv.at[s, k - 1], tp=to)

    sent = []

    def longest(right, ch):
        return 4 if ch == (0 if right else 1) else 3

    for turn in range(4):
        for right, ch in ((True, 0), (False, 0), (False, 1), (True, 1)):
            if turn == 0 and (right, ch) == (False, 1):
                merge(2)
                merge(3)
            k = longest(right, ch) - turn
            if k < 1:
                continue
            place = (z + k) % 8 if right else (z + 8 - k) % 8
            total = block(place, ch)
            if turn > 0:
                ring(right, ch, k + 1).wait_recv()
                total = total + income[slot(right, ch), k].astype(F32)
            outgo[slot(right, ch), k - 1] = total.astype(BF)
            copy = ring(right, ch, k)
            copy.start()
            sent.append(copy)

    value = head_ref[...]
    first = value.astype(BF)
    rest = value - first.astype(F32)
    second = rest.astype(BF)
    third = (rest - second.astype(F32)).astype(BF)
    which = lax.broadcasted_iota(jnp.int32, (16, 512), 0)
    triple = jnp.where(
        which == 0, first.astype(F32),
        jnp.where(which == 1, second.astype(F32), jnp.where(which == 2, third.astype(F32), 0.0)),
    ).astype(BF)
    gaps = []
    for ch in (0, 1):
        total = block(z, ch)
        for right in (True, False):
            ring(right, ch, 1).wait_recv()
            total = total + income[slot(right, ch), 0].astype(F32)
        result = total.astype(BF)
        hidden_out[128 * ch:128 * ch + 128, :] = result
        gaps.append(jnp.sum(dot_nt(triple, result), axis=0, keepdims=True))
    gap = jnp.concatenate(gaps + [jnp.zeros((6, 128), F32)], axis=0)
    gap = jnp.where(sec == 0, gap, -gap)
    own_x = 2 * xh + sec
    gap_own[...] = gap
    gap_x[own_x] = gap
    def gap_far(d):
        return remote(
            gap_own, gap_x.at[own_x], gx_send.at[d - 1], gx_recv.at[d - 1], tp=tp ^ (d // 2), sec=sec ^ (d % 2)
        )

    for d in (1, 2, 3):
        gap_far(d).start()
    for d in (1, 2, 3):
        gap_far(d).wait_recv()
    gap_z[z] = gap_x[0] + gap_x[1] + gap_x[2] + gap_x[3]

    def gap_ring(d):
        return remote(
            gap_z.at[z], gap_z.at[z], gz_send.at[d - 1], gz_recv.at[d - 1], tp=2 * ((z + d) % 8) + xh
        )

    for d in range(1, 8):
        gap_ring(d).start()
    for d in range(1, 8):
        gap_ring(d).wait_recv()
    total = gap_z[0]
    for n in range(1, 8):
        total = total + gap_z[n]
    gap_out[...] = total

    for d in (1, 2, 3):
        gap_far(d).wait_send()
    for d in range(1, 8):
        gap_ring(d).wait_send()
    for copy in sent:
        copy.wait_send()
    for n in range(4):
        lse_copy(n).wait_send()
        o_copy(n).wait_send()


def layer_kernel(
    n_first, n_held, x_hbm, wq_hbm, wkv_hbm, wo_hbm, kv_hbm, len_ref, head_ref, hidden_out, gap_out, *scratch
):
    qkv, near_w, swapped, far_w, kv, kv_sem, *rest = scratch
    first, rest = rest[:n_first], rest[n_first:]
    held, sems = rest[:n_held], rest[n_held:]

    def cache_copy(n):
        rollouts = pl.ds(pl.multiple_of(8 * n, 8), 8)
        return pltpu.make_async_copy(kv_hbm.at[rollouts], kv.at[rollouts], kv_sem.at[n])

    def begin():
        for n in range(8):
            cache_copy(n).start()

    wo, wo2, drain = project(x_hbm, wq_hbm, wkv_hbm, wo_hbm, qkv, near_w, swapped, far_w, begin, *first)
    q_rows, o_own, lse_own, o_got, lse_got, *after = held
    finish(
        qkv, cache_copy, len_ref, wo, wo2, head_ref, hidden_out, gap_out,
        kv, q_rows, o_own, lse_own, o_got, lse_got, near_w, far_w, *after, *sems,
    )
    drain()


def layer(x, wq, wkv, wo, cache, lengths, value_head):
    dma = pltpu.SemaphoreType.DMA
    anywhere = pl.BlockSpec(memory_space=pl.ANY)
    vmem = pl.BlockSpec(memory_space=pltpu.VMEM)
    shared = [
        pltpu.VMEM((2, 256, 640), BF),
        pltpu.VMEM((8, 512, 512), BF),
        pltpu.VMEM((512, 512), BF),
        pltpu.VMEM((8, 512, 512), BF),
        pltpu.VMEM((64, 256, 256), BF),
        dma((8,)),
    ]
    first = [
        pltpu.VMEM((8, 256, 512), BF),
        pltpu.VMEM((2, 1024, 640), BF),
        pltpu.VMEM((2, 4, 128, 640), F32),
        pltpu.VMEM((2, 128, 640), F32),
        pltpu.VMEM((2, 4, 128, 640), BF),
        pltpu.VMEM((2, 4, 128, 640), BF),
        pltpu.VMEM((2, 4, 128, 640), BF),
        pltpu.VMEM((2, 3, 128, 640), BF),
        pltpu.VMEM((2, 128, 640), BF),
        dma((2,)), dma((2,)), dma((4, 2)), dma((4, 2)), dma((4, 2)), dma((4, 2)), dma((2,)), dma((2,)), dma((2,)),
        dma((2, 4)), dma((2, 4)), dma((2, 4)), dma((2, 3)), dma((2,)), dma((2,)), dma((2,)), dma((2, 2)), dma((2,)),
        dma((4,)), dma((4,)), dma((4,)), dma((4,)), dma((1,)), dma((1,)), dma((1,)),
        dma((4,)), dma((4,)), dma((4,)), dma((4,)), dma((1,)),
    ]
    held = [
        pltpu.VMEM((2, 128, 128), F32),
        pltpu.VMEM((2048, 128), BF),
        pltpu.VMEM((16, 1, 128), F32),
        pltpu.VMEM((2048, 128), BF),
        pltpu.VMEM((16, 1, 128), F32),
        pltpu.VMEM((2048, 128), F32),
        pltpu.VMEM((2, 256, 512), BF),
        pltpu.VMEM((4, 4, 128, 512), BF),
        pltpu.VMEM((4, 4, 128, 512), BF),
        pltpu.VMEM((8, 128), F32),
        pltpu.VMEM((4, 8, 128), F32),
        pltpu.VMEM((8, 8, 128), F32),
    ]
    sems = [
        dma((4,)), dma((4,)), dma((4,)), dma((4,)), dma((4, 4)), dma((4, 4)), dma((3,)), dma((3,)), dma((7,)), dma((7,)),
    ]
    return pl.pallas_call(
        functools.partial(layer_kernel, len(first), len(held)),
        out_shape=(jax.ShapeDtypeStruct((256, 512), BF), jax.ShapeDtypeStruct((8, 128), F32)),
        in_specs=[anywhere] * 5 + [pl.BlockSpec(memory_space=pltpu.SMEM), vmem],
        out_specs=(vmem, vmem),
        scratch_shapes=shared + first + held + sems,
        compiler_params=pltpu.CompilerParams(
            collective_id=0, has_side_effects=True, vmem_limit_bytes=60 * MIB
        ),
        name="layer",
    )(x, wq, wkv, wo, cache, lengths, value_head)


def local(layer_in, q_weight, kv_weight, o_weight, kv_cache, cache_lengths, value_head):
    x = layer_in[0].reshape(256, 512)
    hidden, gap = layer(
        x, q_weight[0], kv_weight[0], o_weight[0], kv_cache[0], cache_lengths, value_head.reshape(1, 512)
    )
    hidden_out = hidden.reshape(1, 64, 4, 512)
    own_gap = lax.dynamic_slice_in_dim(gap[:2].reshape(64, 4), 2 * lax.axis_index("sec"), 2, 1)
    return hidden_out, own_gap


def solution(mesh):
    placed = (
        P("sec", "grp", None, "tp"),
        P("sec", "grp", "tp"),
        P("sec", "grp", "tp"),
        P("sec", "tp", "grp"),
        P("sec", "grp", "tp", None),
        P("grp"),
        P("tp"),
    )
    return jax.shard_map(
        local,
        mesh=mesh,
        in_specs=placed,
        out_specs=(P("sec", "grp", None, "tp"), P("grp", "sec")),
        check_vma=False,
    )
```

```python
import functools

import jax
import jax.numpy as jnp
from jax import lax
from jax.experimental import pallas as pl
from jax.experimental.pallas import tpu as pltpu
from jax.sharding import PartitionSpec as P

HD = 128
CACHE = 512
MESH = pl.DeviceIdType.MESH
BF = jnp.bfloat16
F32 = jnp.float32
MIB = 1024 * 1024


def dot(a, b):
    return jnp.dot(a, b, preferred_element_type=F32)


def remote(src, dst, send, recv, **where):
    return pltpu.make_async_remote_copy(
        src_ref=src, dst_ref=dst, send_sem=send, recv_sem=recv, device_id=where, device_id_type=MESH
    )


def places():
    grp, tp = lax.axis_index("grp"), lax.axis_index("tp")
    return grp, tp, grp // 2, grp % 2, tp // 2, tp % 2


class OutputWeights:
    def __init__(self, src, full, y_send, y_recv, c_send, c_recv, own_sem):
        grp, tp, y, c, z, xh = places()
        self.grp, self.c, self.y = grp, c, y
        self.right, self.left = 2 * ((y + 1) % 4) + c, 2 * ((y + 3) % 4) + c
        self.src, self.full = src, full
        self.y_send, self.y_recv, self.c_send, self.c_recv, self.own_sem = y_send, y_recv, c_send, c_recv, own_sem

    def to_core(self, slot, src, place):
        return remote(src, self.full.at[place], self.c_send.at[slot], self.c_recv.at[slot], grp=self.grp ^ 1)

    def from_core(self, slot, place):
        return remote(
            self.full.at[place], self.full.at[place ^ 1], self.c_send.at[slot], self.c_recv.at[slot], grp=self.grp ^ 1
        )

    def one(self, which, place, src=None):
        to = self.right if which == 0 else self.left
        return remote(
            self.full.at[place] if src is None else src, self.full.at[place],
            self.y_send.at[which], self.y_recv.at[which], grp=to,
        )

    def half(self, which, place):
        to = self.right if which == 0 else self.left
        rows = pl.ds(256 * which, 256)
        return remote(
            self.full.at[place, rows], self.full.at[place, rows],
            self.y_send.at[2 + which], self.y_recv.at[2 + which], grp=to,
        )

    def start(self):
        self.own = pltpu.make_async_copy(self.src, self.full.at[self.grp], self.own_sem)
        self.own.start()
        self.sent = [self.one(0, self.grp, self.src), self.one(1, self.grp, self.src), self.to_core(0, self.src, self.grp)]
        for copy in self.sent:
            copy.start()

    def middle(self):
        for which, place in ((0, self.left), (1, self.right)):
            self.one(which, place).wait_recv()
            ahead = self.half(which, place)
            ahead.start()
            over = self.to_core(1 + which, self.full.at[place], place)
            over.start()
            self.sent += [ahead, over]

    def last(self):
        far = 2 * ((self.y + 2) % 4) + self.c
        for which in (0, 1):
            self.half(which, far).wait_recv()
        over = self.to_core(3, self.full.at[far], far)
        over.start()
        self.sent.append(over)

    def finish(self):
        self.own.wait()
        for copy in self.sent:
            copy.wait_send()
        for slot in range(4):
            self.from_core(slot, self.grp).wait_recv()


def project(
    x_hbm, wq_hbm, wkv_hbm, wo_hbm, qkv_out, wo_own, swapped, wo_far, prepare, begin,
    xs, ws, mine, keep, to_core, from_core, to_y, from_y, final,
    perm_send, perm_recv, r_send, r_recv, l_send, l_recv, w_local, w_send, w_recv,
    c_send, c_recv, y_send, y_recv, a_send, a_recv, b_send, b_recv, own_sem,
    g_send, g_recv, h_send, h_recv, g_own, f_send, f_recv, i_send, i_recv, j_send, j_recv, i_own,
):
    grp, tp, y, c, z, xh = places()
    ring_r, ring_l = 2 * ((z + 1) % 8) + xh, 2 * ((z + 7) % 8) + xh
    spot = (z - 2 * y - 4 * xh + 16) % 8
    dst_grp, dst_tp = z, 2 * ((2 * (z // 2) + 2 * y + xh + 4 * c) % 8) + c
    src_grp, src_tp = 2 * (spot // 2) + xh, 2 * grp + spot % 2
    stays = (dst_grp == grp) & (dst_tp == tp)
    moves = jnp.logical_not(stays)

    barrier = pltpu.get_barrier_semaphore()

    def greet(**where):
        pl.semaphore_signal(barrier, inc=1, device_id=where, device_id_type=MESH)

    @pl.when(moves)
    def _():
        greet(grp=dst_grp, tp=dst_tp)
        greet(grp=src_grp, tp=src_tp)

    sec = lax.axis_index("sec")
    greet(tp=tp ^ 1)
    greet(sec=sec ^ 1)
    greet(tp=tp ^ 1, sec=sec ^ 1)
    for d in range(1, 8):
        greet(tp=2 * ((z + d) % 8) + xh)
    greet(grp=grp ^ 1)
    greet(grp=grp ^ 1, tp=tp ^ 1)
    for d in (1, 2, 3):
        greet(grp=2 * ((y + d) % 4) + c)
    prepare()
    pl.semaphore_wait(barrier, jnp.where(moves, 17, 15))

    def rows(ch):
        return pl.ds(128 * ch, 128)

    def perm(ch):
        return remote(
            x_hbm.at[rows(ch)], xs.at[2 * y + xh, rows(ch)], perm_send.at[ch], perm_recv.at[ch], grp=dst_grp, tp=dst_tp
        )

    def perm_local(ch):
        return pltpu.make_async_copy(x_hbm.at[rows(ch)], xs.at[spot, rows(ch)], perm_recv.at[ch])

    for ch in (0, 1):
        pl.when(moves)(lambda ch=ch: perm(ch).start())
        pl.when(stays)(lambda ch=ch: perm_local(ch).start())

    w_out = [
        remote(wq_hbm, ws.at[1, :, pl.ds(0, 512)], w_send.at[0], w_recv.at[0], tp=tp ^ 1),
        remote(wkv_hbm, ws.at[1, :, pl.ds(512, 128)], w_send.at[1], w_recv.at[1], tp=tp ^ 1),
    ]
    w_in = [
        pltpu.make_async_copy(wq_hbm, ws.at[0, :, pl.ds(0, 512)], w_local.at[0]),
        pltpu.make_async_copy(wkv_hbm, ws.at[0, :, pl.ds(512, 128)], w_local.at[1]),
    ]
    for copy in w_out + w_in:
        copy.start()
    wo = OutputWeights(
        wo_hbm.at[:, pl.ds(pl.multiple_of(512 * xh, 512), 512)], wo_own, g_send, g_recv, h_send, h_recv, g_own.at[0]
    )
    wo.start()
    wo2 = OutputWeights(swapped, wo_far, i_send, i_recv, j_send, j_recv, i_own.at[0])
    begin()

    def ring(right, k, ch, place):
        ss, rs, to = (r_send, r_recv, ring_r) if right else (l_send, l_recv, ring_l)
        block = xs.at[place, rows(ch)]
        return remote(block, block, ss.at[k - 1, ch], rs.at[k - 1, ch], tp=to)

    sent = []

    def send(copy):
        copy.start()
        sent.append(copy)

    def travels(right, k, ch):
        return k < 4 or (k == 4 and ch == (0 if right else 1))

    for ch in (0, 1):
        pl.when(moves)(lambda ch=ch: remote(
            x_hbm.at[rows(ch)], xs.at[spot, rows(ch)], perm_send.at[ch], perm_recv.at[ch], grp=dst_grp, tp=dst_tp
        ).wait_recv())
        pl.when(stays)(lambda ch=ch: perm_local(ch).wait())
        for right in (True, False):
            send(ring(right, 1, ch, spot))

    even = spot % 2 == 0
    pair = spot // 2
    order = [
        pair,
        jnp.where(even, pair + 3, pair + 1) % 4,
        jnp.where(even, pair + 1, pair + 3) % 4,
        (pair + 2) % 4,
    ]

    def product(j, yp, half):
        block = pl.ds(pl.multiple_of(128 * half, 128), 128)
        return dot(xs[2 * yp, block, :], ws[j, :512, :]) + dot(xs[2 * yp + 1, block, :], ws[j, 512:, :])

    def core_copy(j, i):
        return remote(to_core.at[j, i], from_core.at[j, i], c_send.at[j, i], c_recv.at[j, i], grp=grp ^ 1)

    def compute(j, i):
        to_core[j, i] = product(j, order[i], c ^ 1).astype(BF)
        send(core_copy(j, i))
        mine[j, i] = product(j, order[i], c)

    def y_copy(j, i, d):
        return remote(
            to_y.at[j, i], from_y.at[j, d - 1], y_send.at[j, i], y_recv.at[j, d - 1],
            grp=2 * ((y + d) % 4) + c,
        )

    def pass_on(j, i):
        core_copy(j, i).wait_recv()
        total = mine[j, i] + from_core[j, i].astype(F32)
        d = (order[i] - y + 4) % 4

        @pl.when(d == 0)
        def _():
            keep[j] = total

        @pl.when(d != 0)
        def _():
            to_y[j, i] = total.astype(BF)
            y_copy(j, i, d).start()

    for copy in w_in:
        copy.wait()
    for k in (1, 2, 3, 4):
        for ch in (0, 1):
            for right in (True, False):
                if not travels(right, k, ch):
                    continue
                place = (spot + 8 - k) % 8 if right else (spot + k) % 8
                ring(right, k, ch, place).wait_recv()
                if k < 4 and travels(right, k + 1, ch):
                    send(ring(right, k + 1, ch, place))
        if k < 4:
            compute(0, k - 1)
        if k == 2:
            pass_on(0, 0)
            wo.middle()
        if k == 3:
            pass_on(0, 1)
            for copy in w_out:
                copy.wait_recv()
            far_cols = pl.ds(pl.multiple_of(512 * (xh ^ 1), 512), 512)
            far = remote(wo_hbm.at[:, far_cols], swapped, f_send.at[0], f_recv.at[0], tp=tp ^ 1)
            far.start()
            compute(1, 0)
            compute(1, 1)
            pass_on(0, 2)
            compute(1, 2)
            wo.last()
            pass_on(1, 0)
            pass_on(1, 1)
    compute(0, 3)
    compute(1, 3)
    pass_on(1, 2)
    pass_on(0, 3)
    pass_on(1, 3)

    near = c == xh

    def place_of(cols, half):
        return qkv_out.at[cols, pl.ds(pl.multiple_of(128 * half, 128), 128)]

    for j in (0, 1):
        total = keep[j]
        for d in (1, 2, 3):
            remote(to_y.at[j, 0], from_y.at[j, d - 1], y_send.at[j, 0], y_recv.at[j, d - 1], grp=grp).wait_recv()
            total = total + from_y[j, d - 1].astype(F32)
        if j == 1:
            far.wait_recv()
            wo2.start()
        final[j] = total.astype(BF)
        spot = place_of(xh ^ j, c)

        @pl.when(near)
        def _():
            pltpu.make_async_copy(final.at[j], spot, own_sem.at[j]).start()

        @pl.when(jnp.logical_not(near))
        def _():
            remote(final.at[j], spot, a_send.at[j], a_recv.at[j], grp=grp ^ 1).start()

        remote(final.at[j], spot, b_send.at[j], b_recv.at[j, c], grp=2 * y + xh, tp=tp ^ 1).start()

    for j in (0, 1):
        spot = place_of(xh ^ j, c)

        @pl.when(near)
        def _():
            pltpu.make_async_copy(final.at[j], spot, own_sem.at[j]).wait()
            remote(final.at[j], place_of(xh ^ j, c ^ 1), a_send.at[j], a_recv.at[j], grp=grp ^ 1).wait_recv()

        @pl.when(jnp.logical_not(near))
        def _():
            remote(final.at[j], spot, a_send.at[j], a_recv.at[j], grp=grp ^ 1).wait_send()
            for half in (0, 1):
                remote(
                    final.at[j], place_of(xh ^ 1 ^ j, half), b_send.at[j], b_recv.at[j, half],
                    grp=2 * y + xh, tp=tp ^ 1,
                ).wait_recv()

    def drain():
        for j in (0, 1):
            remote(
                final.at[j], place_of(xh ^ j, c), b_send.at[j], b_recv.at[j, c], grp=2 * y + xh, tp=tp ^ 1
            ).wait_send()
        for copy in sent:
            copy.wait_send()
        for copy in w_out:
            copy.wait_send()
        for ch in (0, 1):
            pl.when(moves)(lambda ch=ch: perm(ch).wait_send())
        for j in (0, 1):
            for i in range(4):
                d = (order[i] - y + 4) % 4
                pl.when(d != 0)(lambda j=j, i=i, d=d: y_copy(j, i, d).wait_send())
        far.wait_send()

    return wo, wo2, drain


def attend(group, q_ref, kv_ref, len_ref, out_ref, lse_ref, q_rows, xh):
    scale = HD ** -0.5
    lane = lax.broadcasted_iota(jnp.int32, (1, 128), 1)
    pos = lax.broadcasted_iota(jnp.int32, (256, 128), 0)
    lane_roll, lane_step = lane // 32, lane % 32 // 8
    new_row = lax.broadcasted_iota(jnp.int32, (16, 128), 0)
    causal = (new_row // 4 == lane_roll) & (new_row % 4 <= lane_step) & (xh == 0)
    tokens = pl.ds(pl.multiple_of(16 * group, 16), 16)
    for part in (0, 1):
        vals = q_ref[part, tokens, :].astype(F32)
        for head in range(4):
            q_rows[pl.ds(4 * part + head, 16, stride=8), :] = vals[:, 128 * head:128 * head + 128]
    new_key = q_ref[0, tokens, 512:]
    new_val = q_ref[1, tokens, 512:]
    q_t = q_rows[...].T.astype(BF)
    cached = None
    for i in range(4):
        one = dot(kv_ref[4 * group + i, :, :128], q_t)
        cached = one if cached is None else jnp.where(lane_roll == i, one, cached)
    span = jnp.zeros((1, 128), jnp.int32)
    for i in range(4):
        span = jnp.where(lane_roll == i, len_ref[4 * group + i], span)
    visible = pos < span - 256 * xh
    cached = jnp.where(visible, cached * scale, -1e30)
    fresh = jnp.where(causal, dot(new_key, q_t) * scale, -1e30)
    peak = jnp.maximum(jnp.max(cached, axis=0, keepdims=True), jnp.max(fresh, axis=0, keepdims=True))
    cached = jnp.where(visible, jnp.exp(cached - peak), 0.0)
    fresh = jnp.where(causal, jnp.exp(fresh - peak), 0.0)
    total = jnp.sum(cached, axis=0, keepdims=True) + jnp.sum(fresh, axis=0, keepdims=True)
    lse_ref[group] = jnp.where(total > 0.0, peak + jnp.log(jnp.maximum(total, 1e-30)), -1e30)
    inverse = jnp.where(total > 0.0, 1.0 / jnp.maximum(total, 1e-30), 0.0)
    weights = (cached * inverse).T.astype(BF)
    fresh_w = jnp.concatenate([fresh * inverse, jnp.zeros((112, 128), F32)], axis=0).T.astype(BF)
    new_pad = jnp.concatenate([new_val, jnp.zeros((112, 128), BF)], axis=0)
    added = dot(fresh_w, new_pad)
    for i in range(4):
        block = slice(32 * i, 32 * i + 32)
        got = dot(weights[block], kv_ref[4 * group + i, :, 128:]) + added[block]
        out_ref[pl.ds(pl.multiple_of(128 * group + 32 * i, 32), 32), :] = got.astype(BF)


def finish(
    q_ref, cache_copy, len_ref, wo, wo2, heads, head_copy, hidden_out, gap_out,
    kv, q_rows, o_own, lse_own, o_got, lse_got, near_w, far_w, merged, ctx, outgo, income, terms, gap_part, gap_own, gap_x, gap_z,
    o_send, o_recv, s_send, s_recv, ring_send, ring_recv, gx_send, gx_recv, gz_send, gz_recv,
):
    grp, tp, y, c, z, xh = places()
    sec = lax.axis_index("sec")

    def attend_part(n):
        def body(m, carry):
            cache_copy(m).wait()
            for lane in (0, 1):
                attend(2 * m + lane, q_ref, kv, len_ref, o_own, lse_own, q_rows.at[lane], xh)
            return carry

        lax.fori_loop(2 * n, 2 * n + 2, body, 0)

    def o_copy(n):
        block = pl.ds(512 * n, 512)
        return remote(o_own.at[block], o_got.at[block], o_send.at[n], o_recv.at[n], tp=tp ^ 1)

    def lse_copy(n):
        block = pl.ds(4 * n, 4)
        return remote(lse_own.at[block], lse_got.at[block], s_send.at[n], s_recv.at[n], tp=tp ^ 1)

    def merge(n):
        lse_copy(n).wait_recv()
        o_copy(n).wait_recv()
        for m in range(4 * n, 4 * n + 4):
            factor = 1.0 / (1.0 + jnp.exp(lse_got[m] - lse_own[m]))
            factor = jnp.broadcast_to(factor, (128, 128)).T
            block = slice(128 * m, 128 * m + 128)
            own = o_own[block, :].astype(F32)
            got = o_got[block, :].astype(F32)
            merged[block, :] = own * factor + got * (1.0 - factor)
        for part in (0, 1):
            for head in range(4):
                ctx[part, pl.ds(64 * n, 64), pl.ds(128 * head, 128)] = merged[
                    pl.ds(512 * n + 4 * part + head, 64, stride=8), :
                ].astype(BF)

    for n in range(4):
        attend_part(n)
        lse_copy(n).start()
        o_copy(n).start()
        if n == 1:
            wo2.middle()
        if n > 1:
            merge(n - 2)
    wo2.last()
    wo.finish()
    wo2.finish()
    for d in range(1, 8):
        head_copy(d).wait_recv()

    gap_part[...] = jnp.zeros_like(gap_part)

    def block(place, ch):
        total = dot(ctx[xh, 128 * ch:128 * ch + 128, :], near_w[place]) + dot(
            ctx[xh ^ 1, 128 * ch:128 * ch + 128, :], far_w[place]
        )
        valued = total * heads[place]
        gap_part[ch] += valued[:, :128] + valued[:, 128:256] + valued[:, 256:384] + valued[:, 384:]
        return total

    def place_at(right, k):
        return (z + k) % 8 if right else (z + 8 - k) % 8

    def slot(right, ch):
        return 2 * ch + (0 if right else 1)

    def ring(right, ch, k):
        s = slot(right, ch)
        to = 2 * ((z + (1 if right else 7)) % 8) + xh
        return remote(outgo.at[s, k - 1], income.at[s, k - 1], ring_send.at[s, k - 1], ring_recv.at[s, k - 1], tp=to)

    sent = []

    def longest(right, ch):
        return 4 if ch == (0 if right else 1) else 3

    streams = ((True, 0), (False, 0), (False, 1), (True, 1))

    def push(right, ch, k, total):
        outgo[slot(right, ch), k - 1] = total.astype(BF)
        copy = ring(right, ch, k)
        copy.start()
        sent.append(copy)

    for right, ch in streams:
        if (right, ch) == (False, 1):
            merge(2)
            merge(3)
        k = longest(right, ch)
        push(right, ch, k, block(place_at(right, k), ch))
    for ch in (0, 1):
        for right in (True, False):
            for k in range(longest(right, ch) - 1, 0, -1):
                place = place_at(right, k)
                terms[ch, place] = block(place, ch)
        terms[ch, z] = block(z, ch)

    gap = jnp.concatenate(
        [jnp.sum(gap_part[ch].T, axis=0, keepdims=True) for ch in (0, 1)] + [jnp.zeros((6, 128), F32)], axis=0
    )
    gap = jnp.where(sec == 0, gap, -gap)
    own_x = 2 * xh + sec
    gap_own[...] = gap
    gap_x[own_x] = gap

    def gap_far(d):
        return remote(
            gap_own, gap_x.at[own_x], gx_send.at[d - 1], gx_recv.at[d - 1], tp=tp ^ (d // 2), sec=sec ^ (d % 2)
        )

    def gap_ring(d):
        return remote(
            gap_z.at[z], gap_z.at[z], gz_send.at[d - 1], gz_recv.at[d - 1], tp=2 * ((z + d) % 8) + xh
        )

    for d in (1, 2, 3):
        gap_far(d).start()
    for turn in (1, 2, 3):
        for right, ch in streams:
            k = longest(right, ch) - turn
            if k < 1:
                continue
            ring(right, ch, k + 1).wait_recv()
            push(right, ch, k, terms[ch, place_at(right, k)] + income[slot(right, ch), k].astype(F32))
        if turn == 1:
            for d in (1, 2, 3):
                gap_far(d).wait_recv()
            gap_z[z] = gap_x[0] + gap_x[1] + gap_x[2] + gap_x[3]
            for d in range(1, 8):
                gap_ring(d).start()
    for d in range(1, 8):
        gap_ring(d).wait_recv()
    total = gap_z[0]
    for n in range(1, 8):
        total = total + gap_z[n]
    gap_out[...] = total
    for ch in (0, 1):
        total = terms[ch, z]
        for right in (True, False):
            ring(right, ch, 1).wait_recv()
            total = total + income[slot(right, ch), 0].astype(F32)
        hidden_out[32 * ch:32 * ch + 32] = total.reshape(32, 4, 512).astype(BF)

    for d in (1, 2, 3):
        gap_far(d).wait_send()
    for d in range(1, 8):
        gap_ring(d).wait_send()
    for copy in sent:
        copy.wait_send()
    for n in range(4):
        lse_copy(n).wait_send()
        o_copy(n).wait_send()


def layer_kernel(
    n_first, n_held, x_hbm, wq_hbm, wkv_hbm, wo_hbm, kv_hbm, len_ref, head_ref, hidden_out, gap_out, *scratch
):
    qkv, near_w, swapped, far_w, kv, kv_sem, heads, v_send, v_recv, x_split, x_flat, x_sem, *rest = scratch
    grp, tp, y, c, z, xh = places()
    first, rest = rest[:n_first], rest[n_first:]
    held, sems = rest[:n_held], rest[n_held:]

    def cache_copy(n):
        rollouts = pl.ds(pl.multiple_of(8 * n, 8), 8)
        return pltpu.make_async_copy(kv_hbm.at[rollouts], kv.at[rollouts], kv_sem.at[n])

    def head_copy(d):
        return remote(head_ref, heads.at[z], v_send.at[d - 1], v_recv.at[d - 1], tp=2 * ((z + d) % 8) + xh)

    def begin():
        for n in range(8):
            cache_copy(n).start()
        for d in range(1, 8):
            head_copy(d).start()
        heads[z] = head_ref[...]

    def prepare():
        load = pltpu.make_async_copy(x_hbm, x_split, x_sem.at[0])
        load.start()
        load.wait()
        x_flat[...] = x_split[...].astype(F32).reshape(256, 512).astype(BF)

    wo, wo2, drain = project(x_flat, wq_hbm, wkv_hbm, wo_hbm, qkv, near_w, swapped, far_w, prepare, begin, *first)
    q_rows, o_own, lse_own, o_got, lse_got, *after = held
    finish(
        qkv, cache_copy, len_ref, wo, wo2, heads, head_copy, hidden_out, gap_out,
        kv, q_rows, o_own, lse_own, o_got, lse_got, near_w, far_w, *after, *sems,
    )
    drain()
    for d in range(1, 8):
        head_copy(d).wait_send()


def layer(x, wq, wkv, wo, cache, lengths, value_head):
    dma = pltpu.SemaphoreType.DMA
    anywhere = pl.BlockSpec(memory_space=pl.ANY)
    vmem = pl.BlockSpec(memory_space=pltpu.VMEM)
    shared = [
        pltpu.VMEM((2, 256, 640), BF),
        pltpu.VMEM((8, 512, 512), BF),
        pltpu.VMEM((512, 512), BF),
        pltpu.VMEM((8, 512, 512), BF),
        pltpu.VMEM((64, 256, 256), BF),
        dma((8,)),
        pltpu.VMEM((8, 1, 512), F32),
        dma((7,)), dma((7,)),
        pltpu.VMEM((64, 4, 512), BF),
        pltpu.VMEM((256, 512), BF),
        dma((1,)),
    ]
    first = [
        pltpu.VMEM((8, 256, 512), BF),
        pltpu.VMEM((2, 1024, 640), BF),
        pltpu.VMEM((2, 4, 128, 640), F32),
        pltpu.VMEM((2, 128, 640), F32),
        pltpu.VMEM((2, 4, 128, 640), BF),
        pltpu.VMEM((2, 4, 128, 640), BF),
        pltpu.VMEM((2, 4, 128, 640), BF),
        pltpu.VMEM((2, 3, 128, 640), BF),
        pltpu.VMEM((2, 128, 640), BF),
        dma((2,)), dma((2,)), dma((4, 2)), dma((4, 2)), dma((4, 2)), dma((4, 2)), dma((2,)), dma((2,)), dma((2,)),
        dma((2, 4)), dma((2, 4)), dma((2, 4)), dma((2, 3)), dma((2,)), dma((2,)), dma((2,)), dma((2, 2)), dma((2,)),
        dma((4,)), dma((4,)), dma((4,)), dma((4,)), dma((1,)), dma((1,)), dma((1,)),
        dma((4,)), dma((4,)), dma((4,)), dma((4,)), dma((1,)),
    ]
    held = [
        pltpu.VMEM((2, 128, 128), F32),
        pltpu.VMEM((2048, 128), BF),
        pltpu.VMEM((16, 1, 128), F32),
        pltpu.VMEM((2048, 128), BF),
        pltpu.VMEM((16, 1, 128), F32),
        pltpu.VMEM((2048, 128), F32),
        pltpu.VMEM((2, 256, 512), BF),
        pltpu.VMEM((4, 4, 128, 512), BF),
        pltpu.VMEM((4, 4, 128, 512), BF),
        pltpu.VMEM((2, 8, 128, 512), F32),
        pltpu.VMEM((2, 128, 128), F32),
        pltpu.VMEM((8, 128), F32),
        pltpu.VMEM((4, 8, 128), F32),
        pltpu.VMEM((8, 8, 128), F32),
    ]
    sems = [
        dma((4,)), dma((4,)), dma((4,)), dma((4,)), dma((4, 4)), dma((4, 4)), dma((3,)), dma((3,)), dma((7,)), dma((7,)),
    ]
    return pl.pallas_call(
        functools.partial(layer_kernel, len(first), len(held)),
        out_shape=(jax.ShapeDtypeStruct((64, 4, 512), BF), jax.ShapeDtypeStruct((8, 128), F32)),
        in_specs=[anywhere] * 5 + [pl.BlockSpec(memory_space=pltpu.SMEM), vmem],
        out_specs=(vmem, vmem),
        scratch_shapes=shared + first + held + sems,
        compiler_params=pltpu.CompilerParams(
            collective_id=0, has_side_effects=True, vmem_limit_bytes=60 * MIB
        ),
        name="layer",
    )(x, wq, wkv, wo, cache, lengths, value_head)


def local(layer_in, q_weight, kv_weight, o_weight, kv_cache, cache_lengths, value_head):
    hidden, gap = layer(
        layer_in[0], q_weight[0], kv_weight[0], o_weight[0], kv_cache[0], cache_lengths, value_head.reshape(1, 512)
    )
    hidden_out = hidden[None]
    own_gap = lax.dynamic_slice_in_dim(gap[:2].reshape(64, 4), 2 * lax.axis_index("sec"), 2, 1)
    return hidden_out, own_gap


def solution(mesh):
    placed = (
        P("sec", "grp", None, "tp"),
        P("sec", "grp", "tp"),
        P("sec", "grp", "tp"),
        P("sec", "tp", "grp"),
        P("sec", "grp", "tp", None),
        P("grp"),
        P("tp"),
    )
    return jax.shard_map(
        local,
        mesh=mesh,
        in_specs=placed,
        out_specs=(P("sec", "grp", None, "tp"), P("grp", "sec")),
        check_vma=False,
    )
```

```python
import functools

import jax
import jax.numpy as jnp
from jax import lax
from jax.experimental import pallas as pl
from jax.experimental.pallas import tpu as pltpu
from jax.sharding import PartitionSpec as P

HD = 128
CACHE = 512
MESH = pl.DeviceIdType.MESH
BF = jnp.bfloat16
F32 = jnp.float32
MIB = 1024 * 1024


def dot(a, b):
    return jnp.dot(a, b, preferred_element_type=F32)


def remote(src, dst, send, recv, **where):
    return pltpu.make_async_remote_copy(
        src_ref=src, dst_ref=dst, send_sem=send, recv_sem=recv, device_id=where, device_id_type=MESH
    )


def places():
    grp, tp = lax.axis_index("grp"), lax.axis_index("tp")
    return grp, tp, grp // 2, grp % 2, tp // 2, tp % 2


class OutputWeights:
    def __init__(self, src, full, y_send, y_recv, c_send, c_recv, own_sem):
        grp, tp, y, c, z, xh = places()
        self.grp, self.c, self.y = grp, c, y
        self.right, self.left = 2 * ((y + 1) % 4) + c, 2 * ((y + 3) % 4) + c
        self.src, self.full = src, full
        self.y_send, self.y_recv, self.c_send, self.c_recv, self.own_sem = y_send, y_recv, c_send, c_recv, own_sem

    def to_core(self, slot, src, place):
        return remote(src, self.full.at[place], self.c_send.at[slot], self.c_recv.at[slot], grp=self.grp ^ 1)

    def from_core(self, slot, place):
        return remote(
            self.full.at[place], self.full.at[place ^ 1], self.c_send.at[slot], self.c_recv.at[slot], grp=self.grp ^ 1
        )

    def one(self, which, place, src=None):
        to = self.right if which == 0 else self.left
        return remote(
            self.full.at[place] if src is None else src, self.full.at[place],
            self.y_send.at[which], self.y_recv.at[which], grp=to,
        )

    def half(self, which, place):
        to = self.right if which == 0 else self.left
        rows = pl.ds(256 * which, 256)
        return remote(
            self.full.at[place, rows], self.full.at[place, rows],
            self.y_send.at[2 + which], self.y_recv.at[2 + which], grp=to,
        )

    def start(self):
        self.own = pltpu.make_async_copy(self.src, self.full.at[self.grp], self.own_sem)
        self.own.start()
        self.sent = [self.one(0, self.grp, self.src), self.one(1, self.grp, self.src), self.to_core(0, self.src, self.grp)]
        for copy in self.sent:
            copy.start()

    def middle(self):
        for which, place in ((0, self.left), (1, self.right)):
            self.one(which, place).wait_recv()
            ahead = self.half(which, place)
            ahead.start()
            over = self.to_core(1 + which, self.full.at[place], place)
            over.start()
            self.sent += [ahead, over]

    def last(self):
        far = 2 * ((self.y + 2) % 4) + self.c
        for which in (0, 1):
            self.half(which, far).wait_recv()
        over = self.to_core(3, self.full.at[far], far)
        over.start()
        self.sent.append(over)

    def finish(self):
        self.own.wait()
        for copy in self.sent:
            copy.wait_send()
        for slot in range(4):
            self.from_core(slot, self.grp).wait_recv()


def project(
    x_hbm, wq_hbm, wkv_hbm, wo_hbm, qkv_out, wo_own, swapped, wo_far, prepare, begin,
    xs, ws, mine, keep, to_core, from_core, to_y, from_y, final,
    perm_send, perm_recv, r_send, r_recv, l_send, l_recv, w_local, w_send, w_recv,
    c_send, c_recv, y_send, y_recv, a_send, a_recv, b_send, b_recv, own_sem,
    g_send, g_recv, h_send, h_recv, g_own, f_send, f_recv, i_send, i_recv, j_send, j_recv, i_own,
):
    grp, tp, y, c, z, xh = places()
    ring_r, ring_l = 2 * ((z + 1) % 8) + xh, 2 * ((z + 7) % 8) + xh
    spot = (z - 2 * y - 4 * xh + 16) % 8
    dst_grp, dst_tp = z, 2 * ((2 * (z // 2) + 2 * y + xh + 4 * c) % 8) + c
    src_grp, src_tp = 2 * (spot // 2) + xh, 2 * grp + spot % 2
    stays = (dst_grp == grp) & (dst_tp == tp)
    moves = jnp.logical_not(stays)

    barrier = pltpu.get_barrier_semaphore()

    def greet(**where):
        pl.semaphore_signal(barrier, inc=1, device_id=where, device_id_type=MESH)

    @pl.when(moves)
    def _():
        greet(grp=dst_grp, tp=dst_tp)
        greet(grp=src_grp, tp=src_tp)

    sec = lax.axis_index("sec")
    greet(tp=tp ^ 1)
    greet(sec=sec ^ 1)
    greet(tp=tp ^ 1, sec=sec ^ 1)
    for d in range(1, 8):
        greet(tp=2 * ((z + d) % 8) + xh)
    greet(grp=grp ^ 1)
    greet(grp=grp ^ 1, tp=tp ^ 1)
    for d in (1, 2, 3):
        greet(grp=2 * ((y + d) % 4) + c)
    prepare()
    pl.semaphore_wait(barrier, jnp.where(moves, 17, 15))

    def rows(ch):
        return pl.ds(128 * ch, 128)

    def perm(ch):
        return remote(
            x_hbm.at[rows(ch)], xs.at[2 * y + xh, rows(ch)], perm_send.at[ch], perm_recv.at[ch], grp=dst_grp, tp=dst_tp
        )

    def perm_local(ch):
        return pltpu.make_async_copy(x_hbm.at[rows(ch)], xs.at[spot, rows(ch)], perm_recv.at[ch])

    for ch in (0, 1):
        pl.when(moves)(lambda ch=ch: perm(ch).start())
        pl.when(stays)(lambda ch=ch: perm_local(ch).start())

    w_out = [
        remote(wq_hbm, ws.at[1, :, pl.ds(0, 512)], w_send.at[0], w_recv.at[0], tp=tp ^ 1),
        remote(wkv_hbm, ws.at[1, :, pl.ds(512, 128)], w_send.at[1], w_recv.at[1], tp=tp ^ 1),
    ]
    w_in = [
        pltpu.make_async_copy(wq_hbm, ws.at[0, :, pl.ds(0, 512)], w_local.at[0]),
        pltpu.make_async_copy(wkv_hbm, ws.at[0, :, pl.ds(512, 128)], w_local.at[1]),
    ]
    for copy in w_out + w_in:
        copy.start()
    wo = OutputWeights(
        wo_hbm.at[:, pl.ds(pl.multiple_of(512 * xh, 512), 512)], wo_own, g_send, g_recv, h_send, h_recv, g_own.at[0]
    )
    wo.start()
    wo2 = OutputWeights(swapped, wo_far, i_send, i_recv, j_send, j_recv, i_own.at[0])
    begin()

    def ring(right, k, ch, place):
        ss, rs, to = (r_send, r_recv, ring_r) if right else (l_send, l_recv, ring_l)
        block = xs.at[place, rows(ch)]
        return remote(block, block, ss.at[k - 1, ch], rs.at[k - 1, ch], tp=to)

    sent = []

    def send(copy):
        copy.start()
        sent.append(copy)

    def travels(right, k, ch):
        return k < 4 or (k == 4 and ch == (0 if right else 1))

    for ch in (0, 1):
        pl.when(moves)(lambda ch=ch: remote(
            x_hbm.at[rows(ch)], xs.at[spot, rows(ch)], perm_send.at[ch], perm_recv.at[ch], grp=dst_grp, tp=dst_tp
        ).wait_recv())
        pl.when(stays)(lambda ch=ch: perm_local(ch).wait())
        for right in (True, False):
            send(ring(right, 1, ch, spot))

    even = spot % 2 == 0
    pair = spot // 2
    order = [
        pair,
        jnp.where(even, pair + 3, pair + 1) % 4,
        jnp.where(even, pair + 1, pair + 3) % 4,
        (pair + 2) % 4,
    ]

    def product(j, yp, half):
        block = pl.ds(pl.multiple_of(128 * half, 128), 128)
        return dot(xs[2 * yp, block, :], ws[j, :512, :]) + dot(xs[2 * yp + 1, block, :], ws[j, 512:, :])

    def core_copy(j, i):
        return remote(to_core.at[j, i], from_core.at[j, i], c_send.at[j, i], c_recv.at[j, i], grp=grp ^ 1)

    def compute(j, i):
        to_core[j, i] = product(j, order[i], c ^ 1).astype(BF)
        send(core_copy(j, i))
        mine[j, i] = product(j, order[i], c)

    def y_copy(j, i, d):
        return remote(
            to_y.at[j, i], from_y.at[j, d - 1], y_send.at[j, i], y_recv.at[j, d - 1],
            grp=2 * ((y + d) % 4) + c,
        )

    def pass_on(j, i):
        core_copy(j, i).wait_recv()
        total = mine[j, i] + from_core[j, i].astype(F32)
        d = (order[i] - y + 4) % 4

        @pl.when(d == 0)
        def _():
            keep[j] = total

        @pl.when(d != 0)
        def _():
            to_y[j, i] = total.astype(BF)
            y_copy(j, i, d).start()

    for copy in w_in:
        copy.wait()
    for k in (1, 2, 3, 4):
        for ch in (0, 1):
            for right in (True, False):
                if not travels(right, k, ch):
                    continue
                place = (spot + 8 - k) % 8 if right else (spot + k) % 8
                ring(right, k, ch, place).wait_recv()
                if k < 4 and travels(right, k + 1, ch):
                    send(ring(right, k + 1, ch, place))
        if k < 4:
            compute(0, k - 1)
        if k == 2:
            pass_on(0, 0)
            wo.middle()
        if k == 3:
            pass_on(0, 1)
            for copy in w_out:
                copy.wait_recv()
            far_cols = pl.ds(pl.multiple_of(512 * (xh ^ 1), 512), 512)
            far = remote(wo_hbm.at[:, far_cols], swapped, f_send.at[0], f_recv.at[0], tp=tp ^ 1)
            far.start()
            compute(1, 0)
            compute(1, 1)
            pass_on(0, 2)
            compute(1, 2)
            wo.last()
            pass_on(1, 0)
            pass_on(1, 1)
    compute(0, 3)
    compute(1, 3)
    pass_on(1, 2)
    pass_on(0, 3)
    pass_on(1, 3)
    far.wait_recv()
    wo2.start()

    near = c == xh

    def place_of(cols, half):
        return qkv_out.at[cols, pl.ds(pl.multiple_of(128 * half, 128), 128)]

    for j in (0, 1):
        total = keep[j]
        for d in (1, 2, 3):
            remote(to_y.at[j, 0], from_y.at[j, d - 1], y_send.at[j, 0], y_recv.at[j, d - 1], grp=grp).wait_recv()
            total = total + from_y[j, d - 1].astype(F32)
        final[j] = total.astype(BF)
        spot = place_of(xh ^ j, c)

        @pl.when(near)
        def _():
            pltpu.make_async_copy(final.at[j], spot, own_sem.at[j]).start()

        @pl.when(jnp.logical_not(near))
        def _():
            remote(final.at[j], spot, a_send.at[j], a_recv.at[j], grp=grp ^ 1).start()

        remote(final.at[j], spot, b_send.at[j], b_recv.at[j, c], grp=2 * y + xh, tp=tp ^ 1).start()

    for j in (0, 1):
        spot = place_of(xh ^ j, c)

        @pl.when(near)
        def _():
            pltpu.make_async_copy(final.at[j], spot, own_sem.at[j]).wait()
            remote(final.at[j], place_of(xh ^ j, c ^ 1), a_send.at[j], a_recv.at[j], grp=grp ^ 1).wait_recv()

        @pl.when(jnp.logical_not(near))
        def _():
            remote(final.at[j], spot, a_send.at[j], a_recv.at[j], grp=grp ^ 1).wait_send()
            for half in (0, 1):
                remote(
                    final.at[j], place_of(xh ^ 1 ^ j, half), b_send.at[j], b_recv.at[j, half],
                    grp=2 * y + xh, tp=tp ^ 1,
                ).wait_recv()

    def drain():
        for j in (0, 1):
            remote(
                final.at[j], place_of(xh ^ j, c), b_send.at[j], b_recv.at[j, c], grp=2 * y + xh, tp=tp ^ 1
            ).wait_send()
        for copy in sent:
            copy.wait_send()
        for copy in w_out:
            copy.wait_send()
        for ch in (0, 1):
            pl.when(moves)(lambda ch=ch: perm(ch).wait_send())
        for j in (0, 1):
            for i in range(4):
                d = (order[i] - y + 4) % 4
                pl.when(d != 0)(lambda j=j, i=i, d=d: y_copy(j, i, d).wait_send())
        far.wait_send()

    return wo, wo2, drain


def attend(group, q_ref, kv_ref, len_ref, out_ref, lse_ref, q_rows, xh):
    scale = HD ** -0.5
    lane = lax.broadcasted_iota(jnp.int32, (1, 128), 1)
    pos = lax.broadcasted_iota(jnp.int32, (256, 128), 0)
    lane_roll, lane_step = lane // 32, lane % 32 // 8
    new_row = lax.broadcasted_iota(jnp.int32, (16, 128), 0)
    causal = (new_row // 4 == lane_roll) & (new_row % 4 <= lane_step) & (xh == 0)
    tokens = pl.ds(pl.multiple_of(16 * group, 16), 16)
    for part in (0, 1):
        vals = q_ref[part, tokens, :].astype(F32)
        for head in range(4):
            q_rows[pl.ds(4 * part + head, 16, stride=8), :] = vals[:, 128 * head:128 * head + 128]
    new_key = q_ref[0, tokens, 512:]
    new_val = q_ref[1, tokens, 512:]
    q_t = q_rows[...].T.astype(BF)
    cached = None
    for i in range(4):
        one = dot(kv_ref[4 * group + i, :, :128], q_t)
        cached = one if cached is None else jnp.where(lane_roll == i, one, cached)
    span = jnp.zeros((1, 128), jnp.int32)
    for i in range(4):
        span = jnp.where(lane_roll == i, len_ref[4 * group + i], span)
    visible = pos < span - 256 * xh
    cached = jnp.where(visible, cached * scale, -1e30)
    fresh = jnp.where(causal, dot(new_key, q_t) * scale, -1e30)
    peak = jnp.maximum(jnp.max(cached, axis=0, keepdims=True), jnp.max(fresh, axis=0, keepdims=True))
    cached = jnp.where(visible, jnp.exp(cached - peak), 0.0)
    fresh = jnp.where(causal, jnp.exp(fresh - peak), 0.0)
    total = jnp.sum(cached, axis=0, keepdims=True) + jnp.sum(fresh, axis=0, keepdims=True)
    lse_ref[group] = jnp.where(total > 0.0, peak + jnp.log(jnp.maximum(total, 1e-30)), -1e30)
    inverse = jnp.where(total > 0.0, 1.0 / jnp.maximum(total, 1e-30), 0.0)
    weights = (cached * inverse).T.astype(BF)
    fresh_w = jnp.concatenate([fresh * inverse, jnp.zeros((112, 128), F32)], axis=0).T.astype(BF)
    new_pad = jnp.concatenate([new_val, jnp.zeros((112, 128), BF)], axis=0)
    added = dot(fresh_w, new_pad)
    for i in range(4):
        block = slice(32 * i, 32 * i + 32)
        got = dot(weights[block], kv_ref[4 * group + i, :, 128:]) + added[block]
        out_ref[pl.ds(pl.multiple_of(128 * group + 32 * i, 32), 32), :] = got.astype(BF)


def finish(
    q_ref, cache_copy, len_ref, wo, wo2, heads, head_copy, hidden_out, gap_out,
    kv, q_rows, o_own, lse_own, o_got, lse_got, near_w, far_w, merged, ctx, outgo, income, terms, gap_part, gap_own, gap_x, gap_z,
    o_send, o_recv, s_send, s_recv, ring_send, ring_recv, gx_send, gx_recv, gz_send, gz_recv,
):
    grp, tp, y, c, z, xh = places()
    sec = lax.axis_index("sec")

    def attend_part(n):
        def body(m, carry):
            cache_copy(m).wait()
            for lane in (0, 1):
                attend(2 * m + lane, q_ref, kv, len_ref, o_own, lse_own, q_rows.at[lane], xh)
            return carry

        lax.fori_loop(2 * n, 2 * n + 2, body, 0)

    def o_copy(n):
        block = pl.ds(512 * n, 512)
        return remote(o_own.at[block], o_got.at[block], o_send.at[n], o_recv.at[n], tp=tp ^ 1)

    def lse_copy(n):
        block = pl.ds(4 * n, 4)
        return remote(lse_own.at[block], lse_got.at[block], s_send.at[n], s_recv.at[n], tp=tp ^ 1)

    def merge(n):
        lse_copy(n).wait_recv()
        o_copy(n).wait_recv()
        for m in range(4 * n, 4 * n + 4):
            factor = 1.0 / (1.0 + jnp.exp(lse_got[m] - lse_own[m]))
            factor = jnp.broadcast_to(factor, (128, 128)).T
            block = slice(128 * m, 128 * m + 128)
            own = o_own[block, :].astype(F32)
            got = o_got[block, :].astype(F32)
            merged[block, :] = own * factor + got * (1.0 - factor)
        for part in (0, 1):
            for head in range(4):
                ctx[part, pl.ds(64 * n, 64), pl.ds(128 * head, 128)] = merged[
                    pl.ds(512 * n + 4 * part + head, 64, stride=8), :
                ].astype(BF)

    for n in range(4):
        attend_part(n)
        lse_copy(n).start()
        o_copy(n).start()
        if n == 1:
            wo2.middle()
        if n > 1:
            merge(n - 2)
    wo2.last()
    wo.finish()
    wo2.finish()
    for d in range(1, 8):
        head_copy(d).wait_recv()

    gap_part[...] = jnp.zeros_like(gap_part)

    def block(place, ch):
        total = dot(ctx[xh, 128 * ch:128 * ch + 128, :], near_w[place]) + dot(
            ctx[xh ^ 1, 128 * ch:128 * ch + 128, :], far_w[place]
        )
        valued = total * heads[place]
        gap_part[ch] += valued[:, :128] + valued[:, 128:256] + valued[:, 256:384] + valued[:, 384:]
        return total

    def place_at(right, k):
        return (z + k) % 8 if right else (z + 8 - k) % 8

    def slot(right, ch):
        return 2 * ch + (0 if right else 1)

    def ring(right, ch, k):
        s = slot(right, ch)
        to = 2 * ((z + (1 if right else 7)) % 8) + xh
        return remote(outgo.at[s, k - 1], income.at[s, k - 1], ring_send.at[s, k - 1], ring_recv.at[s, k - 1], tp=to)

    sent = []

    def longest(right, ch):
        return 4 if ch == (0 if right else 1) else 3

    streams = ((True, 0), (False, 0), (False, 1), (True, 1))

    def push(right, ch, k, total):
        outgo[slot(right, ch), k - 1] = total.astype(BF)
        copy = ring(right, ch, k)
        copy.start()
        sent.append(copy)

    for right, ch in streams:
        if (right, ch) == (False, 1):
            merge(2)
            merge(3)
        k = longest(right, ch)
        push(right, ch, k, block(place_at(right, k), ch))
    for ch in (0, 1):
        for right in (True, False):
            for k in range(longest(right, ch) - 1, 0, -1):
                place = place_at(right, k)
                terms[ch, place] = block(place, ch)
        terms[ch, z] = block(z, ch)

    gap = jnp.concatenate(
        [jnp.sum(gap_part[ch].T, axis=0, keepdims=True) for ch in (0, 1)] + [jnp.zeros((6, 128), F32)], axis=0
    )
    gap = jnp.where(sec == 0, gap, -gap)
    own_x = 2 * xh + sec
    gap_own[...] = gap
    gap_x[own_x] = gap

    def gap_far(d):
        return remote(
            gap_own, gap_x.at[own_x], gx_send.at[d - 1], gx_recv.at[d - 1], tp=tp ^ (d // 2), sec=sec ^ (d % 2)
        )

    def gap_ring(d):
        return remote(
            gap_z.at[z], gap_z.at[z], gz_send.at[d - 1], gz_recv.at[d - 1], tp=2 * ((z + d) % 8) + xh
        )

    for d in (1, 2, 3):
        gap_far(d).start()
    for turn in (1, 2, 3):
        for right, ch in streams:
            k = longest(right, ch) - turn
            if k < 1:
                continue
            ring(right, ch, k + 1).wait_recv()
            push(right, ch, k, terms[ch, place_at(right, k)] + income[slot(right, ch), k].astype(F32))
        if turn == 1:
            for d in (1, 2, 3):
                gap_far(d).wait_recv()
            gap_z[z] = gap_x[0] + gap_x[1] + gap_x[2] + gap_x[3]
            for d in range(1, 8):
                gap_ring(d).start()
    for d in range(1, 8):
        gap_ring(d).wait_recv()
    total = gap_z[0]
    for n in range(1, 8):
        total = total + gap_z[n]
    gap_out[...] = total
    for ch in (0, 1):
        total = terms[ch, z]
        for right in (True, False):
            ring(right, ch, 1).wait_recv()
            total = total + income[slot(right, ch), 0].astype(F32)
        hidden_out[32 * ch:32 * ch + 32] = total.reshape(32, 4, 512).astype(BF)

    for d in (1, 2, 3):
        gap_far(d).wait_send()
    for d in range(1, 8):
        gap_ring(d).wait_send()
    for copy in sent:
        copy.wait_send()
    for n in range(4):
        lse_copy(n).wait_send()
        o_copy(n).wait_send()


def layer_kernel(
    n_first, n_held, x_hbm, wq_hbm, wkv_hbm, wo_hbm, kv_hbm, len_ref, head_ref, hidden_out, gap_out, *scratch
):
    qkv, near_w, swapped, far_w, kv, kv_sem, heads, v_send, v_recv, x_split, x_flat, x_sem, *rest = scratch
    grp, tp, y, c, z, xh = places()
    first, rest = rest[:n_first], rest[n_first:]
    held, sems = rest[:n_held], rest[n_held:]

    def cache_copy(n):
        rollouts = pl.ds(pl.multiple_of(8 * n, 8), 8)
        return pltpu.make_async_copy(kv_hbm.at[rollouts], kv.at[rollouts], kv_sem.at[n])

    def head_copy(d):
        return remote(head_ref, heads.at[z], v_send.at[d - 1], v_recv.at[d - 1], tp=2 * ((z + d) % 8) + xh)

    def begin():
        for n in range(8):
            cache_copy(n).start()
        for d in range(1, 8):
            head_copy(d).start()
        heads[z] = head_ref[...]

    def prepare():
        load = pltpu.make_async_copy(x_hbm, x_split, x_sem.at[0])
        load.start()
        load.wait()
        x_flat[...] = x_split[...].astype(F32).reshape(256, 512).astype(BF)

    wo, wo2, drain = project(x_flat, wq_hbm, wkv_hbm, wo_hbm, qkv, near_w, swapped, far_w, prepare, begin, *first)
    q_rows, o_own, lse_own, o_got, lse_got, *after = held
    finish(
        qkv, cache_copy, len_ref, wo, wo2, heads, head_copy, hidden_out, gap_out,
        kv, q_rows, o_own, lse_own, o_got, lse_got, near_w, far_w, *after, *sems,
    )
    drain()
    for d in range(1, 8):
        head_copy(d).wait_send()


def layer(x, wq, wkv, wo, cache, lengths, value_head):
    dma = pltpu.SemaphoreType.DMA
    anywhere = pl.BlockSpec(memory_space=pl.ANY)
    vmem = pl.BlockSpec(memory_space=pltpu.VMEM)
    shared = [
        pltpu.VMEM((2, 256, 640), BF),
        pltpu.VMEM((8, 512, 512), BF),
        pltpu.VMEM((512, 512), BF),
        pltpu.VMEM((8, 512, 512), BF),
        pltpu.VMEM((64, 256, 256), BF),
        dma((8,)),
        pltpu.VMEM((8, 1, 512), F32),
        dma((7,)), dma((7,)),
        pltpu.VMEM((64, 4, 512), BF),
        pltpu.VMEM((256, 512), BF),
        dma((1,)),
    ]
    first = [
        pltpu.VMEM((8, 256, 512), BF),
        pltpu.VMEM((2, 1024, 640), BF),
        pltpu.VMEM((2, 4, 128, 640), F32),
        pltpu.VMEM((2, 128, 640), F32),
        pltpu.VMEM((2, 4, 128, 640), BF),
        pltpu.VMEM((2, 4, 128, 640), BF),
        pltpu.VMEM((2, 4, 128, 640), BF),
        pltpu.VMEM((2, 3, 128, 640), BF),
        pltpu.VMEM((2, 128, 640), BF),
        dma((2,)), dma((2,)), dma((4, 2)), dma((4, 2)), dma((4, 2)), dma((4, 2)), dma((2,)), dma((2,)), dma((2,)),
        dma((2, 4)), dma((2, 4)), dma((2, 4)), dma((2, 3)), dma((2,)), dma((2,)), dma((2,)), dma((2, 2)), dma((2,)),
        dma((4,)), dma((4,)), dma((4,)), dma((4,)), dma((1,)), dma((1,)), dma((1,)),
        dma((4,)), dma((4,)), dma((4,)), dma((4,)), dma((1,)),
    ]
    held = [
        pltpu.VMEM((2, 128, 128), F32),
        pltpu.VMEM((2048, 128), BF),
        pltpu.VMEM((16, 1, 128), F32),
        pltpu.VMEM((2048, 128), BF),
        pltpu.VMEM((16, 1, 128), F32),
        pltpu.VMEM((2048, 128), F32),
        pltpu.VMEM((2, 256, 512), BF),
        pltpu.VMEM((4, 4, 128, 512), BF),
        pltpu.VMEM((4, 4, 128, 512), BF),
        pltpu.VMEM((2, 8, 128, 512), F32),
        pltpu.VMEM((2, 128, 128), F32),
        pltpu.VMEM((8, 128), F32),
        pltpu.VMEM((4, 8, 128), F32),
        pltpu.VMEM((8, 8, 128), F32),
    ]
    sems = [
        dma((4,)), dma((4,)), dma((4,)), dma((4,)), dma((4, 4)), dma((4, 4)), dma((3,)), dma((3,)), dma((7,)), dma((7,)),
    ]
    return pl.pallas_call(
        functools.partial(layer_kernel, len(first), len(held)),
        out_shape=(jax.ShapeDtypeStruct((64, 4, 512), BF), jax.ShapeDtypeStruct((8, 128), F32)),
        in_specs=[anywhere] * 5 + [pl.BlockSpec(memory_space=pltpu.SMEM), vmem],
        out_specs=(vmem, vmem),
        scratch_shapes=shared + first + held + sems,
        compiler_params=pltpu.CompilerParams(
            collective_id=0, has_side_effects=True, vmem_limit_bytes=60 * MIB
        ),
        name="layer",
    )(x, wq, wkv, wo, cache, lengths, value_head)


def local(layer_in, q_weight, kv_weight, o_weight, kv_cache, cache_lengths, value_head):
    hidden, gap = layer(
        layer_in[0], q_weight[0], kv_weight[0], o_weight[0], kv_cache[0], cache_lengths, value_head.reshape(1, 512)
    )
    hidden_out = hidden[None]
    own_gap = lax.dynamic_slice_in_dim(gap[:2].reshape(64, 4), 2 * lax.axis_index("sec"), 2, 1)
    return hidden_out, own_gap


def solution(mesh):
    placed = (
        P("sec", "grp", None, "tp"),
        P("sec", "grp", "tp"),
        P("sec", "grp", "tp"),
        P("sec", "tp", "grp"),
        P("sec", "grp", "tp", None),
        P("grp"),
        P("tp"),
    )
    return jax.shard_map(
        local,
        mesh=mesh,
        in_specs=placed,
        out_specs=(P("sec", "grp", None, "tp"), P("grp", "sec")),
        check_vma=False,
    )
```

```python
import functools

import jax
import jax.numpy as jnp
from jax import lax
from jax.experimental import pallas as pl
from jax.experimental.pallas import tpu as pltpu
from jax.sharding import PartitionSpec as P

HD = 128
CACHE = 512
MESH = pl.DeviceIdType.MESH
BF = jnp.bfloat16
F32 = jnp.float32
MIB = 1024 * 1024


def dot(a, b):
    return jnp.dot(a, b, preferred_element_type=F32)


def remote(src, dst, send, recv, **where):
    return pltpu.make_async_remote_copy(
        src_ref=src, dst_ref=dst, send_sem=send, recv_sem=recv, device_id=where, device_id_type=MESH
    )


def places():
    grp, tp = lax.axis_index("grp"), lax.axis_index("tp")
    return grp, tp, grp // 2, grp % 2, tp // 2, tp % 2


class OutputWeights:
    def __init__(self, src, full, y_send, y_recv, c_send, c_recv, own_sem):
        grp, tp, y, c, z, xh = places()
        self.grp, self.c, self.y = grp, c, y
        self.right, self.left = 2 * ((y + 1) % 4) + c, 2 * ((y + 3) % 4) + c
        self.src, self.full = src, full
        self.y_send, self.y_recv, self.c_send, self.c_recv, self.own_sem = y_send, y_recv, c_send, c_recv, own_sem

    def to_core(self, slot, src, place):
        return remote(src, self.full.at[place], self.c_send.at[slot], self.c_recv.at[slot], grp=self.grp ^ 1)

    def from_core(self, slot, place):
        return remote(
            self.full.at[place], self.full.at[place ^ 1], self.c_send.at[slot], self.c_recv.at[slot], grp=self.grp ^ 1
        )

    def one(self, which, place, src=None):
        to = self.right if which == 0 else self.left
        return remote(
            self.full.at[place] if src is None else src, self.full.at[place],
            self.y_send.at[which], self.y_recv.at[which], grp=to,
        )

    def half(self, which, place):
        to = self.right if which == 0 else self.left
        rows = pl.ds(256 * which, 256)
        return remote(
            self.full.at[place, rows], self.full.at[place, rows],
            self.y_send.at[2 + which], self.y_recv.at[2 + which], grp=to,
        )

    def start(self):
        self.own = pltpu.make_async_copy(self.src, self.full.at[self.grp], self.own_sem)
        self.own.start()
        self.sent = [self.one(0, self.grp, self.src), self.one(1, self.grp, self.src), self.to_core(0, self.src, self.grp)]
        for copy in self.sent:
            copy.start()

    def middle(self):
        for which, place in ((0, self.left), (1, self.right)):
            self.one(which, place).wait_recv()
            ahead = self.half(which, place)
            ahead.start()
            over = self.to_core(1 + which, self.full.at[place], place)
            over.start()
            self.sent += [ahead, over]

    def last(self):
        far = 2 * ((self.y + 2) % 4) + self.c
        for which in (0, 1):
            self.half(which, far).wait_recv()
        over = self.to_core(3, self.full.at[far], far)
        over.start()
        self.sent.append(over)

    def finish(self):
        self.own.wait()
        for copy in self.sent:
            copy.wait_send()
        for slot in range(4):
            self.from_core(slot, self.grp).wait_recv()


def project(
    x_hbm, wq_hbm, wkv_hbm, wo_hbm, qkv_out, wo_own, swapped, wo_far, prepare, begin,
    xs, ws, mine, keep, to_core, from_core, to_y, from_y, final,
    perm_send, perm_recv, r_send, r_recv, l_send, l_recv, w_local, w_send, w_recv,
    c_send, c_recv, y_send, y_recv, a_send, a_recv, b_send, b_recv, own_sem,
    g_send, g_recv, h_send, h_recv, g_own, f_send, f_recv, i_send, i_recv, j_send, j_recv, i_own,
):
    grp, tp, y, c, z, xh = places()
    ring_r, ring_l = 2 * ((z + 1) % 8) + xh, 2 * ((z + 7) % 8) + xh
    spot = (z - 2 * y - 4 * xh + 16) % 8
    dst_grp, dst_tp = z, 2 * ((2 * (z // 2) + 2 * y + xh + 4 * c) % 8) + c
    src_grp, src_tp = 2 * (spot // 2) + xh, 2 * grp + spot % 2
    stays = (dst_grp == grp) & (dst_tp == tp)
    moves = jnp.logical_not(stays)

    barrier = pltpu.get_barrier_semaphore()

    def greet(**where):
        pl.semaphore_signal(barrier, inc=1, device_id=where, device_id_type=MESH)

    @pl.when(moves)
    def _():
        greet(grp=dst_grp, tp=dst_tp)
        greet(grp=src_grp, tp=src_tp)

    sec = lax.axis_index("sec")
    greet(tp=tp ^ 1)
    greet(sec=sec ^ 1)
    greet(tp=tp ^ 1, sec=sec ^ 1)
    for d in range(1, 8):
        greet(tp=2 * ((z + d) % 8) + xh)
    greet(grp=grp ^ 1)
    greet(grp=grp ^ 1, tp=tp ^ 1)
    for d in (1, 2, 3):
        greet(grp=2 * ((y + d) % 4) + c)
    prepare()
    pl.semaphore_wait(barrier, jnp.where(moves, 17, 15))

    def rows(ch):
        return pl.ds(128 * ch, 128)

    def perm(ch):
        return remote(
            x_hbm.at[rows(ch)], xs.at[2 * y + xh, rows(ch)], perm_send.at[ch], perm_recv.at[ch], grp=dst_grp, tp=dst_tp
        )

    def perm_local(ch):
        return pltpu.make_async_copy(x_hbm.at[rows(ch)], xs.at[spot, rows(ch)], perm_recv.at[ch])

    for ch in (0, 1):
        pl.when(moves)(lambda ch=ch: perm(ch).start())
        pl.when(stays)(lambda ch=ch: perm_local(ch).start())

    w_out = [
        remote(wq_hbm, ws.at[1, :, pl.ds(0, 512)], w_send.at[0], w_recv.at[0], tp=tp ^ 1),
        remote(wkv_hbm, ws.at[1, :, pl.ds(512, 128)], w_send.at[1], w_recv.at[1], tp=tp ^ 1),
    ]
    w_in = [
        pltpu.make_async_copy(wq_hbm, ws.at[0, :, pl.ds(0, 512)], w_local.at[0]),
        pltpu.make_async_copy(wkv_hbm, ws.at[0, :, pl.ds(512, 128)], w_local.at[1]),
    ]
    for copy in w_out + w_in:
        copy.start()
    wo = OutputWeights(
        wo_hbm.at[:, pl.ds(pl.multiple_of(512 * xh, 512), 512)], wo_own, g_send, g_recv, h_send, h_recv, g_own.at[0]
    )
    wo2 = OutputWeights(swapped, wo_far, i_send, i_recv, j_send, j_recv, i_own.at[0])
    begin()

    def ring(right, k, ch, place):
        ss, rs, to = (r_send, r_recv, ring_r) if right else (l_send, l_recv, ring_l)
        block = xs.at[place, rows(ch)]
        return remote(block, block, ss.at[k - 1, ch], rs.at[k - 1, ch], tp=to)

    sent = []

    def send(copy):
        copy.start()
        sent.append(copy)

    def travels(right, k, ch):
        return k < 4 or (k == 4 and ch == (0 if right else 1))

    for ch in (0, 1):
        pl.when(moves)(lambda ch=ch: remote(
            x_hbm.at[rows(ch)], xs.at[spot, rows(ch)], perm_send.at[ch], perm_recv.at[ch], grp=dst_grp, tp=dst_tp
        ).wait_recv())
        pl.when(stays)(lambda ch=ch: perm_local(ch).wait())
        for right in (True, False):
            send(ring(right, 1, ch, spot))

    wo.start()
    even = spot % 2 == 0
    pair = spot // 2
    order = [
        pair,
        jnp.where(even, pair + 3, pair + 1) % 4,
        jnp.where(even, pair + 1, pair + 3) % 4,
        (pair + 2) % 4,
    ]

    def product(j, yp, half):
        block = pl.ds(pl.multiple_of(128 * half, 128), 128)
        return dot(xs[2 * yp, block, :], ws[j, :512, :]) + dot(xs[2 * yp + 1, block, :], ws[j, 512:, :])

    def core_copy(j, i):
        return remote(to_core.at[j, i], from_core.at[j, i], c_send.at[j, i], c_recv.at[j, i], grp=grp ^ 1)

    def compute(j, i):
        to_core[j, i] = product(j, order[i], c ^ 1).astype(BF)
        send(core_copy(j, i))
        mine[j, i] = product(j, order[i], c)

    def y_copy(j, i, d):
        return remote(
            to_y.at[j, i], from_y.at[j, d - 1], y_send.at[j, i], y_recv.at[j, d - 1],
            grp=2 * ((y + d) % 4) + c,
        )

    def pass_on(j, i):
        core_copy(j, i).wait_recv()
        total = mine[j, i] + from_core[j, i].astype(F32)
        d = (order[i] - y + 4) % 4

        @pl.when(d == 0)
        def _():
            keep[j] = total

        @pl.when(d != 0)
        def _():
            to_y[j, i] = total.astype(BF)
            y_copy(j, i, d).start()

    for copy in w_in:
        copy.wait()
    for k in (1, 2, 3, 4):
        for ch in (0, 1):
            for right in (True, False):
                if not travels(right, k, ch):
                    continue
                place = (spot + 8 - k) % 8 if right else (spot + k) % 8
                ring(right, k, ch, place).wait_recv()
                if k < 4 and travels(right, k + 1, ch):
                    send(ring(right, k + 1, ch, place))
        if k < 4:
            compute(0, k - 1)
        if k == 2:
            pass_on(0, 0)
            wo.middle()
        if k == 3:
            pass_on(0, 1)
            for copy in w_out:
                copy.wait_recv()
            far_cols = pl.ds(pl.multiple_of(512 * (xh ^ 1), 512), 512)
            far = remote(wo_hbm.at[:, far_cols], swapped, f_send.at[0], f_recv.at[0], tp=tp ^ 1)
            far.start()
            compute(1, 0)
            compute(1, 1)
            pass_on(0, 2)
            compute(1, 2)
            wo.last()
            pass_on(1, 0)
            pass_on(1, 1)
    compute(0, 3)
    compute(1, 3)
    pass_on(1, 2)
    pass_on(0, 3)
    pass_on(1, 3)
    far.wait_recv()
    wo2.start()

    near = c == xh

    def place_of(cols, half):
        return qkv_out.at[cols, pl.ds(pl.multiple_of(128 * half, 128), 128)]

    for j in (0, 1):
        total = keep[j]
        for d in (1, 2, 3):
            remote(to_y.at[j, 0], from_y.at[j, d - 1], y_send.at[j, 0], y_recv.at[j, d - 1], grp=grp).wait_recv()
            total = total + from_y[j, d - 1].astype(F32)
        final[j] = total.astype(BF)
        spot = place_of(xh ^ j, c)

        @pl.when(near)
        def _():
            pltpu.make_async_copy(final.at[j], spot, own_sem.at[j]).start()

        @pl.when(jnp.logical_not(near))
        def _():
            remote(final.at[j], spot, a_send.at[j], a_recv.at[j], grp=grp ^ 1).start()

        remote(final.at[j], spot, b_send.at[j], b_recv.at[j, c], grp=2 * y + xh, tp=tp ^ 1).start()

    for j in (0, 1):
        spot = place_of(xh ^ j, c)

        @pl.when(near)
        def _():
            pltpu.make_async_copy(final.at[j], spot, own_sem.at[j]).wait()
            remote(final.at[j], place_of(xh ^ j, c ^ 1), a_send.at[j], a_recv.at[j], grp=grp ^ 1).wait_recv()

        @pl.when(jnp.logical_not(near))
        def _():
            remote(final.at[j], spot, a_send.at[j], a_recv.at[j], grp=grp ^ 1).wait_send()
            for half in (0, 1):
                remote(
                    final.at[j], place_of(xh ^ 1 ^ j, half), b_send.at[j], b_recv.at[j, half],
                    grp=2 * y + xh, tp=tp ^ 1,
                ).wait_recv()

    def drain():
        for j in (0, 1):
            remote(
                final.at[j], place_of(xh ^ j, c), b_send.at[j], b_recv.at[j, c], grp=2 * y + xh, tp=tp ^ 1
            ).wait_send()
        for copy in sent:
            copy.wait_send()
        for copy in w_out:
            copy.wait_send()
        for ch in (0, 1):
            pl.when(moves)(lambda ch=ch: perm(ch).wait_send())
        for j in (0, 1):
            for i in range(4):
                d = (order[i] - y + 4) % 4
                pl.when(d != 0)(lambda j=j, i=i, d=d: y_copy(j, i, d).wait_send())
        far.wait_send()

    return wo, wo2, drain


def attend(group, q_ref, kv_ref, len_ref, out_ref, lse_ref, q_rows, xh):
    scale = HD ** -0.5
    lane = lax.broadcasted_iota(jnp.int32, (1, 128), 1)
    pos = lax.broadcasted_iota(jnp.int32, (256, 128), 0)
    lane_roll, lane_step = lane // 32, lane % 32 // 8
    new_row = lax.broadcasted_iota(jnp.int32, (16, 128), 0)
    causal = (new_row // 4 == lane_roll) & (new_row % 4 <= lane_step) & (xh == 0)
    tokens = pl.ds(pl.multiple_of(16 * group, 16), 16)
    for part in (0, 1):
        vals = q_ref[part, tokens, :].astype(F32)
        for head in range(4):
            q_rows[pl.ds(4 * part + head, 16, stride=8), :] = vals[:, 128 * head:128 * head + 128]
    new_key = q_ref[0, tokens, 512:]
    new_val = q_ref[1, tokens, 512:]
    q_t = q_rows[...].T.astype(BF)
    cached = None
    for i in range(4):
        one = dot(kv_ref[4 * group + i, :, :128], q_t)
        cached = one if cached is None else jnp.where(lane_roll == i, one, cached)
    span = jnp.zeros((1, 128), jnp.int32)
    for i in range(4):
        span = jnp.where(lane_roll == i, len_ref[4 * group + i], span)
    visible = pos < span - 256 * xh
    cached = jnp.where(visible, cached * scale, -1e30)
    fresh = jnp.where(causal, dot(new_key, q_t) * scale, -1e30)
    peak = jnp.maximum(jnp.max(cached, axis=0, keepdims=True), jnp.max(fresh, axis=0, keepdims=True))
    cached = jnp.where(visible, jnp.exp(cached - peak), 0.0)
    fresh = jnp.where(causal, jnp.exp(fresh - peak), 0.0)
    total = jnp.sum(cached, axis=0, keepdims=True) + jnp.sum(fresh, axis=0, keepdims=True)
    lse_ref[group] = jnp.where(total > 0.0, peak + jnp.log(jnp.maximum(total, 1e-30)), -1e30)
    inverse = jnp.where(total > 0.0, 1.0 / jnp.maximum(total, 1e-30), 0.0)
    weights = (cached * inverse).T.astype(BF)
    fresh_w = jnp.concatenate([fresh * inverse, jnp.zeros((112, 128), F32)], axis=0).T.astype(BF)
    new_pad = jnp.concatenate([new_val, jnp.zeros((112, 128), BF)], axis=0)
    added = dot(fresh_w, new_pad)
    for i in range(4):
        block = slice(32 * i, 32 * i + 32)
        got = dot(weights[block], kv_ref[4 * group + i, :, 128:]) + added[block]
        out_ref[pl.ds(pl.multiple_of(128 * group + 32 * i, 32), 32), :] = got.astype(BF)


def finish(
    q_ref, cache_copy, len_ref, wo, wo2, heads, head_copy, hidden_out, gap_out,
    kv, q_rows, o_own, lse_own, o_got, lse_got, near_w, far_w, merged, ctx, outgo, income, terms, gap_part, gap_own, gap_x, gap_z,
    o_send, o_recv, s_send, s_recv, ring_send, ring_recv, gx_send, gx_recv, gz_send, gz_recv,
):
    grp, tp, y, c, z, xh = places()
    sec = lax.axis_index("sec")

    def attend_part(n):
        def body(m, carry):
            cache_copy(m).wait()
            for lane in (0, 1):
                attend(2 * m + lane, q_ref, kv, len_ref, o_own, lse_own, q_rows.at[lane], xh)
            return carry

        lax.fori_loop(2 * n, 2 * n + 2, body, 0)

    def o_copy(n):
        block = pl.ds(512 * n, 512)
        return remote(o_own.at[block], o_got.at[block], o_send.at[n], o_recv.at[n], tp=tp ^ 1)

    def lse_copy(n):
        block = pl.ds(4 * n, 4)
        return remote(lse_own.at[block], lse_got.at[block], s_send.at[n], s_recv.at[n], tp=tp ^ 1)

    def merge(n):
        lse_copy(n).wait_recv()
        o_copy(n).wait_recv()
        for m in range(4 * n, 4 * n + 4):
            factor = 1.0 / (1.0 + jnp.exp(lse_got[m] - lse_own[m]))
            factor = jnp.broadcast_to(factor, (128, 128)).T
            block = slice(128 * m, 128 * m + 128)
            own = o_own[block, :].astype(F32)
            got = o_got[block, :].astype(F32)
            merged[block, :] = own * factor + got * (1.0 - factor)
        for part in (0, 1):
            for head in range(4):
                ctx[part, pl.ds(64 * n, 64), pl.ds(128 * head, 128)] = merged[
                    pl.ds(512 * n + 4 * part + head, 64, stride=8), :
                ].astype(BF)

    for n in range(4):
        attend_part(n)
        lse_copy(n).start()
        o_copy(n).start()
        if n == 1:
            wo2.middle()
        if n > 1:
            merge(n - 2)
    wo2.last()
    wo.finish()
    wo2.finish()
    for d in range(1, 8):
        head_copy(d).wait_recv()

    gap_part[...] = jnp.zeros_like(gap_part)

    def block(place, ch):
        total = dot(ctx[xh, 128 * ch:128 * ch + 128, :], near_w[place]) + dot(
            ctx[xh ^ 1, 128 * ch:128 * ch + 128, :], far_w[place]
        )
        valued = total * heads[place]
        gap_part[ch] += valued[:, :128] + valued[:, 128:256] + valued[:, 256:384] + valued[:, 384:]
        return total

    def place_at(right, k):
        return (z + k) % 8 if right else (z + 8 - k) % 8

    def slot(right, ch):
        return 2 * ch + (0 if right else 1)

    def ring(right, ch, k):
        s = slot(right, ch)
        to = 2 * ((z + (1 if right else 7)) % 8) + xh
        return remote(outgo.at[s, k - 1], income.at[s, k - 1], ring_send.at[s, k - 1], ring_recv.at[s, k - 1], tp=to)

    sent = []

    def longest(right, ch):
        return 4 if ch == (0 if right else 1) else 3

    streams = ((True, 0), (False, 0), (False, 1), (True, 1))

    def push(right, ch, k, total):
        outgo[slot(right, ch), k - 1] = total.astype(BF)
        copy = ring(right, ch, k)
        copy.start()
        sent.append(copy)

    for right, ch in streams:
        if (right, ch) == (False, 1):
            merge(2)
            merge(3)
        k = longest(right, ch)
        push(right, ch, k, block(place_at(right, k), ch))
    for ch in (0, 1):
        for right in (True, False):
            for k in range(longest(right, ch) - 1, 0, -1):
                place = place_at(right, k)
                terms[ch, place] = block(place, ch)
        terms[ch, z] = block(z, ch)

    gap = jnp.concatenate(
        [jnp.sum(gap_part[ch].T, axis=0, keepdims=True) for ch in (0, 1)] + [jnp.zeros((6, 128), F32)], axis=0
    )
    gap = jnp.where(sec == 0, gap, -gap)
    own_x = 2 * xh + sec
    gap_own[...] = gap
    gap_x[own_x] = gap

    def gap_far(d):
        return remote(
            gap_own, gap_x.at[own_x], gx_send.at[d - 1], gx_recv.at[d - 1], tp=tp ^ (d // 2), sec=sec ^ (d % 2)
        )

    def gap_ring(d):
        return remote(
            gap_z.at[z], gap_z.at[z], gz_send.at[d - 1], gz_recv.at[d - 1], tp=2 * ((z + d) % 8) + xh
        )

    for d in (1, 2, 3):
        gap_far(d).start()
    for turn in (1, 2, 3):
        for right, ch in streams:
            k = longest(right, ch) - turn
            if k < 1:
                continue
            ring(right, ch, k + 1).wait_recv()
            push(right, ch, k, terms[ch, place_at(right, k)] + income[slot(right, ch), k].astype(F32))
        if turn == 1:
            for d in (1, 2, 3):
                gap_far(d).wait_recv()
            gap_z[z] = gap_x[0] + gap_x[1] + gap_x[2] + gap_x[3]
            for d in range(1, 8):
                gap_ring(d).start()
    for d in range(1, 8):
        gap_ring(d).wait_recv()
    total = gap_z[0]
    for n in range(1, 8):
        total = total + gap_z[n]
    gap_out[...] = total
    for ch in (0, 1):
        total = terms[ch, z]
        for right in (True, False):
            ring(right, ch, 1).wait_recv()
            total = total + income[slot(right, ch), 0].astype(F32)
        hidden_out[32 * ch:32 * ch + 32] = total.reshape(32, 4, 512).astype(BF)

    for d in (1, 2, 3):
        gap_far(d).wait_send()
    for d in range(1, 8):
        gap_ring(d).wait_send()
    for copy in sent:
        copy.wait_send()
    for n in range(4):
        lse_copy(n).wait_send()
        o_copy(n).wait_send()


def layer_kernel(
    n_first, n_held, x_hbm, wq_hbm, wkv_hbm, wo_hbm, kv_hbm, len_ref, head_ref, hidden_out, gap_out, *scratch
):
    qkv, near_w, swapped, far_w, kv, kv_sem, heads, v_send, v_recv, x_split, x_flat, x_sem, *rest = scratch
    grp, tp, y, c, z, xh = places()
    first, rest = rest[:n_first], rest[n_first:]
    held, sems = rest[:n_held], rest[n_held:]

    def cache_copy(n):
        rollouts = pl.ds(pl.multiple_of(8 * n, 8), 8)
        return pltpu.make_async_copy(kv_hbm.at[rollouts], kv.at[rollouts], kv_sem.at[n])

    def head_copy(d):
        return remote(head_ref, heads.at[z], v_send.at[d - 1], v_recv.at[d - 1], tp=2 * ((z + d) % 8) + xh)

    def begin():
        for n in range(8):
            cache_copy(n).start()
        for d in range(1, 8):
            head_copy(d).start()
        heads[z] = head_ref[...]

    def prepare():
        load = pltpu.make_async_copy(x_hbm, x_split, x_sem.at[0])
        load.start()
        load.wait()
        x_flat[...] = x_split[...].astype(F32).reshape(256, 512).astype(BF)

    wo, wo2, drain = project(x_flat, wq_hbm, wkv_hbm, wo_hbm, qkv, near_w, swapped, far_w, prepare, begin, *first)
    q_rows, o_own, lse_own, o_got, lse_got, *after = held
    finish(
        qkv, cache_copy, len_ref, wo, wo2, heads, head_copy, hidden_out, gap_out,
        kv, q_rows, o_own, lse_own, o_got, lse_got, near_w, far_w, *after, *sems,
    )
    drain()
    for d in range(1, 8):
        head_copy(d).wait_send()


def layer(x, wq, wkv, wo, cache, lengths, value_head):
    dma = pltpu.SemaphoreType.DMA
    anywhere = pl.BlockSpec(memory_space=pl.ANY)
    vmem = pl.BlockSpec(memory_space=pltpu.VMEM)
    shared = [
        pltpu.VMEM((2, 256, 640), BF),
        pltpu.VMEM((8, 512, 512), BF),
        pltpu.VMEM((512, 512), BF),
        pltpu.VMEM((8, 512, 512), BF),
        pltpu.VMEM((64, 256, 256), BF),
        dma((8,)),
        pltpu.VMEM((8, 1, 512), F32),
        dma((7,)), dma((7,)),
        pltpu.VMEM((64, 4, 512), BF),
        pltpu.VMEM((256, 512), BF),
        dma((1,)),
    ]
    first = [
        pltpu.VMEM((8, 256, 512), BF),
        pltpu.VMEM((2, 1024, 640), BF),
        pltpu.VMEM((2, 4, 128, 640), F32),
        pltpu.VMEM((2, 128, 640), F32),
        pltpu.VMEM((2, 4, 128, 640), BF),
        pltpu.VMEM((2, 4, 128, 640), BF),
        pltpu.VMEM((2, 4, 128, 640), BF),
        pltpu.VMEM((2, 3, 128, 640), BF),
        pltpu.VMEM((2, 128, 640), BF),
        dma((2,)), dma((2,)), dma((4, 2)), dma((4, 2)), dma((4, 2)), dma((4, 2)), dma((2,)), dma((2,)), dma((2,)),
        dma((2, 4)), dma((2, 4)), dma((2, 4)), dma((2, 3)), dma((2,)), dma((2,)), dma((2,)), dma((2, 2)), dma((2,)),
        dma((4,)), dma((4,)), dma((4,)), dma((4,)), dma((1,)), dma((1,)), dma((1,)),
        dma((4,)), dma((4,)), dma((4,)), dma((4,)), dma((1,)),
    ]
    held = [
        pltpu.VMEM((2, 128, 128), F32),
        pltpu.VMEM((2048, 128), BF),
        pltpu.VMEM((16, 1, 128), F32),
        pltpu.VMEM((2048, 128), BF),
        pltpu.VMEM((16, 1, 128), F32),
        pltpu.VMEM((2048, 128), F32),
        pltpu.VMEM((2, 256, 512), BF),
        pltpu.VMEM((4, 4, 128, 512), BF),
        pltpu.VMEM((4, 4, 128, 512), BF),
        pltpu.VMEM((2, 8, 128, 512), F32),
        pltpu.VMEM((2, 128, 128), F32),
        pltpu.VMEM((8, 128), F32),
        pltpu.VMEM((4, 8, 128), F32),
        pltpu.VMEM((8, 8, 128), F32),
    ]
    sems = [
        dma((4,)), dma((4,)), dma((4,)), dma((4,)), dma((4, 4)), dma((4, 4)), dma((3,)), dma((3,)), dma((7,)), dma((7,)),
    ]
    return pl.pallas_call(
        functools.partial(layer_kernel, len(first), len(held)),
        out_shape=(jax.ShapeDtypeStruct((64, 4, 512), BF), jax.ShapeDtypeStruct((8, 128), F32)),
        in_specs=[anywhere] * 5 + [pl.BlockSpec(memory_space=pltpu.SMEM), vmem],
        out_specs=(vmem, vmem),
        scratch_shapes=shared + first + held + sems,
        compiler_params=pltpu.CompilerParams(
            collective_id=0, has_side_effects=True, vmem_limit_bytes=60 * MIB
        ),
        name="layer",
    )(x, wq, wkv, wo, cache, lengths, value_head)


def local(layer_in, q_weight, kv_weight, o_weight, kv_cache, cache_lengths, value_head):
    hidden, gap = layer(
        layer_in[0], q_weight[0], kv_weight[0], o_weight[0], kv_cache[0], cache_lengths, value_head.reshape(1, 512)
    )
    hidden_out = hidden[None]
    own_gap = lax.dynamic_slice_in_dim(gap[:2].reshape(64, 4), 2 * lax.axis_index("sec"), 2, 1)
    return hidden_out, own_gap


def solution(mesh):
    placed = (
        P("sec", "grp", None, "tp"),
        P("sec", "grp", "tp"),
        P("sec", "grp", "tp"),
        P("sec", "tp", "grp"),
        P("sec", "grp", "tp", None),
        P("grp"),
        P("tp"),
    )
    return jax.shard_map(
        local,
        mesh=mesh,
        in_specs=placed,
        out_specs=(P("sec", "grp", None, "tp"), P("grp", "sec")),
        check_vma=False,
    )
```
